256 devices in a mesh: band: 8 (over y, x_lo), mesh: 32 (over x_hi, z, core).
Axes of the slice: x: 4 (x_hi: 2, x_lo: 2; x = x_hi * 2 + x_lo), y: 4, z: 8, core: 2. Of those that a mesh axis runs over, the one named last changes fastest.
Arguments:
- bands_in: float32 [32768, 2048], P('mesh', 'band'), may hold values from -6 to 6
- cell_ham: float32 [96, 512, 512], P('mesh'), may hold values from -0.25 to 0.25
- cell_nodes: int32 [96, 512], P('mesh'), may hold values from 0 to 1023
- left_face: int32 [32, 128], P('mesh'), may hold values from 0 to 1023, as said below
- right_face: int32 [32, 128], P('mesh'), may hold values from 0 to 1023, as said below
- proj_values: float32 [1024, 18, 128], P('mesh'), may hold values from -0.375 to 0.375
- proj_nodes: int32 [1024, 128], P('mesh'), may hold values from 0 to 1023
- slot_owner: int32 [1024, 1], P('mesh'), may hold values from 0 to 31; in each aligned block of 32 rows (0 to 31, 32 to 63, ...) at most 2 rows name the same one
- slot_atom: int32 [1024], P('mesh'), may hold values from 0 to 15
- coupling: float32 [512, 18, 18], P('mesh'), may hold values from -1.5 to 1.5
- node_weight: float32 [32768], P('mesh'), may hold values from 0.00012207031 to 0.0012207031
- filter_center: float32 [1], replicated, may hold values from 0.5 to 1.5
- filter_half: float32 [1], replicated, may hold values from 2 to 3
Outputs:
- filtered: float32 [32768, 2048], P('mesh', 'band')
- margin: float32 [2048, 2048], P('band', 'mesh')
The draws below stay inside these ranges and needn't reach their ends.
Inputs may be any that keep to these rules, and one draw needn't show every extreme that they name: `cell_nodes`: local node numbers within the cell's part. In each part the 128 entries of left_face and of right_face are all distinct and the two lists share no node; entry i of part p's right_face is the node that entry i of part p + 1's left_face names. `right_face`: see left_face. `proj_nodes`: local node numbers within the slot's part. `slot_owner`: among the 32 slots of one part, at most 2 name the same owner.
All inputs are finite; a program needn't handle non-finite values.
Results may differ from the reference program's by a relative error of at most 0.0002.
Values sent between devices are 32-bit elements; how exact they have to be, the bound alone decides.
A program may use at most 64 MiB of HBM per device.

```python
import math
import jax
import jax.numpy as jnp
import numpy as np
from jax import lax

NODE_CELL = 512
PROJ = 18
SUPPORT = 128
CELLS_DEV = 3
SLOTS_DEV = 32
NODES_DEV = 1024
FACE = 128
ATOMS_OWN = 16
MESH_PARTS = 32
CAP = 2
NODES = 32768
CELLS = 96
SLOTS = 1024
ATOMS = 512
BANDS = 2048


def face_lists(key):
    part_keys = jax.random.split(jax.random.fold_in(key, 1117), MESH_PARTS)
    shuffled = jax.vmap(lambda single: jax.random.permutation(single, NODES_DEV))(part_keys)
    return (shuffled[:, :FACE].astype(jnp.int32), shuffled[:, FACE:2 * FACE].astype(jnp.int32))


def draw_left_face(key, part):
    return face_lists(key)[0]


def draw_right_face(key, part):
    return face_lists(key)[1]


def place_ends(result, rng, least, largest):
    index_at = [jax.random.randint(jax.random.fold_in(rng, axis), (), 0, length) for axis, length in enumerate(result.shape)]
    widest = result.shape.index(max(result.shape))
    next_to = index_at[:widest] + [(index_at[widest] + 1) % result.shape[widest]] + index_at[widest + 1:]
    return result.at[tuple(index_at)].set(least).at[tuple(next_to)].set(largest)


def shard_levels(stream_key, extent, cuts, low, largest):
    gain = 1.0
    for axis_at, blocks in cuts:
        heights = jax.random.uniform(jax.random.fold_in(jax.random.fold_in(stream_key, 6), axis_at), (blocks,), jnp.float32, low / len(cuts), largest / len(cuts))
        gain = gain * jnp.repeat(jnp.exp(heights), extent[axis_at] // blocks).reshape((-1,) + (1,) * (len(extent) - 1 - axis_at))
    return gain


def deal_out(rng, own, number, rows, count, top, limit, skew):
    ranking = jax.random.permutation(rng, count)
    crowded, common = portions_of(count, rows * top, limit, skew, True), portions_of(count, rows * top, limit, skew, False)
    places = jnp.arange(count)

    def named(sizes, offset_by):
        used = int((sizes > 0).sum())
        fixed = max(1, used // 4)
        passed = fixed + (places - fixed + offset_by * (used - fixed)) % max(1, count - fixed)
        return jnp.zeros((count,), jnp.int32).at[ranking[jnp.where(places < fixed, places, passed)]].set(jnp.asarray(sizes, jnp.int32))

    sizes = jnp.where(number % 4 == 0, named(crowded, number // 4), named(common, number - number // 4 - 1))
    mixed = jax.random.permutation(jax.random.fold_in(own, 3), count)
    giver, sink = mixed[0:count // 2 * 2:2], mixed[1:count // 2 * 2:2]
    slack = jnp.minimum(sizes[giver] - 1, limit - sizes[sink]) // 2
    slack = jnp.where((giver == ranking[0]) | (sink == ranking[0]) | (sizes[sink] == 0), 0, jnp.maximum(slack, 0))
    passed = jax.random.randint(jax.random.fold_in(own, 4), (count // 2,), 0, 1 << 20) % (slack + 1)
    sizes = sizes.at[giver].add(-passed).at[sink].add(passed)
    members = jnp.searchsorted(jnp.cumsum(sizes), jnp.arange(rows * top), side="right").astype(jnp.int32)
    listing = members.reshape(top, rows).T
    listing = listing[jax.random.permutation(jax.random.fold_in(own, 1), rows)]
    offset_by = jax.random.randint(jax.random.fold_in(own, 2), (rows, 1), 0, top)
    return jnp.take_along_axis(listing, (jnp.arange(top)[None, :] + offset_by) % top, axis=1)


def portions_of(number_of, total, limit, lean, full):
    loads = [(1 << 20) // math.isqrt(grade ** lean) + 1 for grade in range(1, number_of + 1)]
    largest = limit if full else min(limit, max(-(-total // number_of), total * loads[0] // sum(loads)))
    least = 1 if total - largest >= number_of - 1 else 0
    counts, rest = [largest] + [least] * (number_of - 1), total - largest - least * (number_of - 1)
    while rest > 0:
        movable = [i for i in range(1, number_of) if counts[i] < largest] or [i for i in range(1, number_of) if counts[i] < limit]
        whole, left = sum([loads[i] for i in movable]), rest
        for i in movable:
            more = min(limit - counts[i], max(1, left * loads[i] // whole), rest)
            counts[i] = counts[i] + more
            rest = rest - more
    return np.array(counts)


def normal_values(own_key, extent, scale, most, shards=(), held_as=jnp.bfloat16):
    drawn = scale * jax.random.normal(own_key, extent, jnp.float32)
    if shards:
        drawn = drawn * shard_levels(own_key, extent, shards, -0.22, 0.18)
    return jnp.clip(drawn, -most, most).astype(held_as)


def setup_inputs(seed: int = 0) -> dict:
    streams_of = jax.random.split(jax.random.key(seed), 14)
    bands_in = normal_values(streams_of[0], (NODES, BANDS), 1.0, 6.0, ((0, 32), (1, 8)), jnp.float32)
    cell_ham = normal_values(streams_of[1], (CELLS, NODE_CELL, NODE_CELL), NODE_CELL ** -0.5, 0.25, ((0, 32),), jnp.float32)
    cell_nodes = place_ends(jax.random.randint(streams_of[2], (CELLS, NODE_CELL), 0, NODES_DEV), jax.random.fold_in(streams_of[2], 1), 0, NODES_DEV - 1).astype(jnp.int32)
    left_face = draw_left_face(jax.random.fold_in(streams_of[13], 71), 0)
    right_face = draw_right_face(jax.random.fold_in(streams_of[13], 71), 0)
    proj_values = normal_values(streams_of[5], (SLOTS, PROJ, SUPPORT), (PROJ * SUPPORT // 8) ** -0.5, 0.375, ((0, 32),), jnp.float32)
    proj_nodes = place_ends(jax.random.randint(streams_of[6], (SLOTS, SUPPORT), 0, NODES_DEV), jax.random.fold_in(streams_of[6], 1), 0, NODES_DEV - 1).astype(jnp.int32)
    slot_owner_keys = jax.random.split(jax.random.fold_in(streams_of[7], 1), SLOTS // SLOTS_DEV)
    slot_owner_turns = jax.random.permutation(jax.random.fold_in(streams_of[7], 3), SLOTS // SLOTS_DEV)
    slot_owner = jax.vmap(lambda own, number: deal_out(jax.random.fold_in(streams_of[7], 2), own, number, SLOTS_DEV, MESH_PARTS, 1, CAP, 2))(slot_owner_keys, slot_owner_turns).reshape((SLOTS, 1))
    slot_atom = place_ends(jax.random.randint(streams_of[8], (SLOTS,), 0, ATOMS_OWN), jax.random.fold_in(streams_of[8], 1), 0, ATOMS_OWN - 1).astype(jnp.int32)
    coupling = normal_values(streams_of[9], (ATOMS, PROJ, PROJ), PROJ ** -0.5, 1.5, ((0, 32),), jnp.float32)
    node_weight = jnp.clip(jnp.exp(math.log(0.0012207031) - 2.3025851 * jax.random.uniform(streams_of[10], (NODES,), jnp.float32) ** shard_levels(streams_of[10], (NODES,), ((0, 32),), -0.2, 0.2)), 0.00012207031, 0.0012207031)
    filter_center = jnp.clip(jax.random.uniform(streams_of[11], (1,), jnp.float32, 0.5, 1.5), 0.5, 1.5)
    filter_half = jnp.clip(jax.random.uniform(streams_of[12], (1,), jnp.float32, 2.0, 3.0), 2.0, 3.0)
    return {"bands_in": bands_in, "cell_ham": cell_ham, "cell_nodes": cell_nodes, "left_face": left_face, "right_face": right_face, "proj_values": proj_values, "proj_nodes": proj_nodes, "slot_owner": slot_owner, "slot_atom": slot_atom, "coupling": coupling, "node_weight": node_weight, "filter_center": filter_center, "filter_half": filter_half}


precise = lax.Precision.HIGHEST


def cell_apply(vectors, hamiltonians, node_lists):
    columns = vectors.shape[1]
    gathered = vectors[node_lists]
    product = jnp.einsum("cij,cjb->cib", hamiltonians, gathered, precision=precise)
    return jnp.zeros_like(vectors).at[node_lists.reshape(-1)].add(product.reshape(-1, columns))


def gather_rows(part_block, row_list):
    return part_block[row_list]


def add_faces(part_block, right_rows, from_right, left_rows, from_left):
    return part_block.at[right_rows].add(from_right).at[left_rows].add(from_left)


def coefficients(packed):
    vectors, values, node_rows = packed
    return jnp.einsum("spn,snb->spb", values, vectors[node_rows], precision=precise)


def spread_back(packed):
    values, node_rows, returned = packed
    spreading = jnp.einsum("spn,spb->snb", values, returned, precision=precise)
    empty = jnp.zeros((NODES_DEV, BANDS), jnp.float32)
    return empty.at[node_rows.reshape(-1)].add(spreading.reshape(-1, BANDS))


def reference(bands_in, cell_ham, cell_nodes, left_face, right_face, proj_values, proj_nodes, slot_owner, slot_atom, coupling, node_weight, filter_center, filter_half):
    hamiltonians = cell_ham.reshape(MESH_PARTS, CELLS_DEV, NODE_CELL, NODE_CELL)
    node_lists = cell_nodes.reshape(MESH_PARTS, CELLS_DEV, NODE_CELL)
    projector_values = proj_values.reshape(MESH_PARTS, SLOTS_DEV, PROJ, SUPPORT)
    projector_nodes = proj_nodes.reshape(MESH_PARTS, SLOTS_DEV, SUPPORT)
    segment = (slot_owner[:, 0] * ATOMS_OWN + slot_atom).astype(jnp.int32)
    boundary = jnp.zeros((1, FACE, BANDS), jnp.float32)

    def scaled(vectors):
        blocks = vectors.reshape(MESH_PARTS, NODES_DEV, BANDS)
        cell_part = lax.map(lambda packed: cell_apply(packed[0], packed[1], packed[2]), (blocks, hamiltonians, node_lists))
        left_values = jax.vmap(gather_rows)(cell_part, left_face)
        right_values = jax.vmap(gather_rows)(cell_part, right_face)
        from_right = jnp.concatenate([left_values[1:], boundary], axis=0)
        from_left = jnp.concatenate([boundary, right_values[:-1]], axis=0)
        assembled = jax.vmap(add_faces)(cell_part, right_face, from_right, left_face, from_left)
        coefficient = lax.map(coefficients, (blocks, projector_values, projector_nodes)).reshape(SLOTS, PROJ, BANDS)
        totals = jax.ops.segment_sum(coefficient, segment, num_segments=ATOMS)
        applied = jnp.einsum("apq,aqb->apb", coupling, totals, precision=precise)
        returned = applied[segment].reshape(MESH_PARTS, SLOTS_DEV, PROJ, BANDS)
        nonlocal_part = lax.map(spread_back, (projector_values, projector_nodes, returned))
        operator = (assembled + nonlocal_part).reshape(NODES, BANDS)
        return (operator - filter_center[0] * vectors) / filter_half[0]

    first_term = scaled(bands_in)
    second = 2.0 * scaled(first_term) - bands_in
    filtered = 2.0 * scaled(second) - first_term
    weighted = filtered * node_weight[:, None]
    margin = jnp.dot(weighted.T, filtered, precision=precise)
    return (filtered, margin)
```

```python
import functools

import jax
import jax.numpy as jnp
from jax import lax
from jax.experimental import pallas as pl
from jax.experimental.pallas import tpu as pltpu
from jax.sharding import PartitionSpec as P

MESH = pl.DeviceIdType.MESH
precise = lax.Precision.HIGHEST
f32, bf16, i32 = jnp.float32, jnp.bfloat16, jnp.int32

PARTS = 32
NODES = 1024
COLS = 256
SLOTS = 32
PROJ = 18
PADDED = 24
ATOMS = 16
CELLS = 3
CELL = 512
FACE = 128
MAIN = PARTS * 32
ROWS = MAIN + PARTS * 8
TERMS = ATOMS * PADDED
BLOCK = 256


def mm(a, b):
    return jnp.dot(a, b, preferred_element_type=f32)


def split(x):
    high = x.astype(bf16)
    return high, (x - high.astype(f32)).astype(bf16)


def iota(shape, dim):
    return lax.broadcasted_iota(i32, shape, dim)


def hot(mask):
    return jnp.where(mask, 1.0, 0.0).astype(bf16)


def rows_at(index, size=BLOCK):
    return pl.ds(pl.multiple_of(index * size, size), size)


def loop(count, body):
    def step(i, carry):
        body(i)
        return carry

    lax.fori_loop(0, count, step, 0)


def filter_kernel(
    scalars,
    bands_in,
    cell_ham,
    cell_rows,
    cell_cols,
    face_row,
    face_col,
    proj_values,
    proj_cols,
    row_source,
    labels,
    coupling,
    filtered,
    b24,
    b24h,
    b24l,
    b8h,
    b8l,
    bth,
    btl,
    gat,
    sca,
    fgat,
    fsca,
    member,
    memt,
    cbh,
    cbl,
    vh,
    vl,
    xh,
    xl,
    gh,
    gl,
    ph,
    plo,
    cells,
    previous,
    out1,
    in1,
    out2,
    in2,
    lab_in,
    face_out,
    face_in,
    s1,
    r1,
    s2,
    r2,
    sl,
    rl,
    sf,
    rf,
):
    me = lax.axis_index("mesh")
    band = lax.axis_index("band")
    centre, half = scalars[0, 0], scalars[0, 1]

    def peer(k):
        return lax.rem(me + k, PARTS)

    face_in[...] = jnp.zeros_like(face_in)
    barrier = pltpu.get_barrier_semaphore()

    def greet(k):
        pl.semaphore_signal(barrier, inc=1, device_id=(band, peer(k + 1)), device_id_type=MESH)

    loop(PARTS - 1, greet)

    b24[...] = jnp.zeros_like(b24)
    for s in range(SLOTS):
        spread = hot(proj_cols[:, s : s + 1] == iota((128, NODES), 1))
        high, low = split(proj_values[s])
        b24[s * PADDED : s * PADDED + PROJ, :] = mm(high, spread) + mm(low, spread)
    high, low = split(b24[...])
    b24h[...] = high
    b24l[...] = low

    def place(i):
        at = rows_at(i)
        chosen = hot(row_source[at, :] == iota((BLOCK, SLOTS * PADDED), 1))
        b8h[at, :] = mm(chosen, b24h[...]).astype(bf16)
        b8l[at, :] = mm(chosen, b24l[...]).astype(bf16)

    loop(ROWS // BLOCK, place)

    def set_field(x):
        high, low = split(x)
        vh[...] = high
        vl[...] = low

    filtered[...] = bands_in[...]
    previous[...] = bands_in[...]
    set_field(bands_in[...])

    def copy_to(source, target, send, receive, o):
        return pltpu.make_async_remote_copy(
            source.at[o],
            target.at[me],
            send.at[o],
            receive.at[me],
            device_id=(band, o),
            device_id_type=MESH,
        )

    def arrival(source, target, send, receive, q):
        return pltpu.make_async_remote_copy(
            source.at[q],
            target.at[q],
            send.at[q],
            receive.at[q],
            device_id=(band, q),
            device_id_type=MESH,
        )

    def exchange(rows_of, out, target, send, receive, wait=None):
        tail = rows_of(MAIN // BLOCK)
        first = lax.rem(iota((BLOCK, 128), 0), 8) < 4
        out[:, 64:72, :] = jnp.where(first, tail[:, :128], tail[:, 128:]).reshape(PARTS, 8, 128)

        def group(t):
            g = lax.rem(me // 8 + 1 + t, 4)
            block = rows_of(g)
            out[pl.ds(g * 8, 8), 0:32, :] = block[:, :128].reshape(8, 32, 128)
            out[pl.ds(g * 8, 8), 32:64, :] = block[:, 128:].reshape(8, 32, 128)

            def one(i):
                o = g * 8 + lax.rem(me + i, 8)

                @pl.when(o != me)
                def _():
                    copy_to(out, target, send, receive, o).start()

            loop(8, one)

        loop(4, group)
        target[me] = out[me]

    def collect(out, target, send, receive):
        def one(k):
            arrival(out, target, send, receive, peer(k + 1)).wait_recv()

        loop(PARTS - 1, one)
        main = target[:, 0:64, :]
        left = main[:, 0:32, :].reshape(MAIN, 128)
        right = main[:, 32:64, :].reshape(MAIN, 128)
        tail = target[:, 64:72, :].reshape(BLOCK, 128)
        first = lax.rem(iota((BLOCK, 128), 0), 8) < 4
        for columns, top, keep in ((0, left, first), (128, right, jnp.logical_not(first))):
            high, low = split(top)
            xh[0:MAIN, columns : columns + 128] = high
            xl[0:MAIN, columns : columns + 128] = low
            high, low = split(jnp.where(keep, tail, 0.0))
            xh[MAIN:ROWS, columns : columns + 128] = high
            xl[MAIN:ROWS, columns : columns + 128] = low

    def sent(out, target, send, receive):
        def one(k):
            arrival(out, target, send, receive, peer(k + 1)).wait_send()

        loop(PARTS - 1, one)

    def coefficient(i):
        at = rows_at(i)
        return mm(b8h[at, :], vh[...]) + (mm(b8h[at, :], vl[...]) + mm(b8l[at, :], vh[...]))

    pl.semaphore_wait(barrier, PARTS - 1)

    def tell(k):
        copy_to(labels, lab_in, sl, rl, peer(k + 1)).start()

    loop(PARTS - 1, tell)
    exchange(coefficient, out1, in1, s1, r1)
    lab_in[me] = labels[me]

    for c in range(CELLS):
        for h in range(2):
            gat[c * CELL + h * BLOCK : c * CELL + (h + 1) * BLOCK, :] = hot(
                cell_cols[h * BLOCK : (h + 1) * BLOCK, c : c + 1] == iota((BLOCK, NODES), 1)
            )
    for i in range(NODES // BLOCK):
        row = iota((BLOCK, CELL), 0) + i * BLOCK
        for c in range(CELLS):
            sca[i * BLOCK : (i + 1) * BLOCK, c * CELL : (c + 1) * CELL] = hot(row == cell_rows[c : c + 1, :])
        fsca[i * BLOCK : (i + 1) * BLOCK, :] = hot(row[:, :256] == face_row[...])
    fgat[...] = hot(face_col[...] == iota((2 * FACE, NODES), 1))
    for i in range(ROWS // BLOCK):
        at = slice(i * BLOCK, (i + 1) * BLOCK)
        bth[:, at] = b8h[at, :].astype(f32).T.astype(bf16)
        btl[:, at] = b8l[at, :].astype(f32).T.astype(bf16)
    repeat = hot(iota((PADDED, TERMS), 0) == lax.rem(iota((PADDED, TERMS), 1), PADDED))
    same = iota((TERMS, TERMS), 0) // PADDED == iota((TERMS, TERMS), 1) // PADDED
    high, low = split(coupling[...])
    cbh[...] = jnp.where(same, mm(high, repeat), 0.0).astype(bf16)
    cbl[...] = jnp.where(same, mm(low, repeat), 0.0).astype(bf16)

    def told(k):
        arrival(labels, lab_in, sl, rl, peer(k + 1)).wait()

    loop(PARTS - 1, told)
    col = iota((128, ROWS), 1)
    index = jnp.where(col < MAIN, lax.rem(col, 32), 32 + lax.rem(col, 8))
    place_of = hot(iota((128, ROWS), 0) == index)
    named = mm(lab_in[...].reshape(PARTS * 8, 128).astype(bf16), place_of)
    col = iota((PARTS * 8, ROWS), 1)
    source = jnp.where(col < MAIN, col // 32, (col - MAIN) // 8)
    atom = jnp.sum(jnp.where(iota((PARTS * 8, ROWS), 0) == source * 8, named, 0.0), axis=0, keepdims=True)
    col = iota((1, ROWS), 1)
    number = jnp.where(col < MAIN, lax.rem(col, 32), 32 + lax.rem(col, 4))
    key = jnp.where(atom < 0.0, -1, atom.astype(i32) * PADDED + lax.rem(number, PROJ))
    for i in range(ROWS // BLOCK):
        at = slice(i * BLOCK, (i + 1) * BLOCK)
        mask = jnp.where(iota((TERMS, BLOCK), 0) == key[:, at], 1.0, 0.0)
        member[:, at] = mask.astype(bf16)
        memt[at, :] = mask.T.astype(bf16)

    def returned(i):
        at = rows_at(i)
        return mm(memt[at, :], ph[0:TERMS, :]) + mm(memt[at, :], plo[0:TERMS, :])

    def face_copy(step, low, other):
        source = face_out.at[pl.ds(0 if low else FACE, FACE)]
        target = face_in.at[step, pl.ds(FACE if low else 0, FACE)]
        side = 0 if low else 1
        return pltpu.make_async_remote_copy(
            source, target, sf.at[side], rf.at[step, 1 - side], device_id=(band, other), device_id_type=MESH
        )

    def face_wait(step, low, other):
        source = face_out.at[pl.ds(0 if low else FACE, FACE)]
        target = face_in.at[step, pl.ds(0 if low else FACE, FACE)]
        side = 0 if low else 1
        return pltpu.make_async_remote_copy(
            source, target, sf.at[side], rf.at[step, side], device_id=(band, other), device_id_type=MESH
        )

    def degree(step):
        gain = jnp.where(step == 0, 1.0, 2.0) / half
        keep = jnp.where(step == 0, 0.0, 1.0)

        def pick(i):
            at = rows_at(i)
            gh[at, :] = mm(gat[at, :], vh[...]).astype(bf16)
            gl[at, :] = mm(gat[at, :], vl[...]).astype(bf16)

        loop(CELLS * CELL // BLOCK, pick)

        def multiply(c):
            at = rows_at(c, CELL)
            for h in range(2):
                high, low = split(cell_ham[c, h * BLOCK : (h + 1) * BLOCK, :])
                result = mm(high, gh[at, :]) + (mm(high, gl[at, :]) + mm(low, gh[at, :]))
                high, low = split(result)
                to = pl.ds(pl.multiple_of(c * CELL + h * BLOCK, BLOCK), BLOCK)
                ph[to, :] = high
                plo[to, :] = low

        loop(CELLS, multiply)

        def add(i):
            at = rows_at(i)
            cells[at, :] = mm(sca[at, :], ph[...]) + mm(sca[at, :], plo[...])

        loop(NODES // BLOCK, add)
        high, low = split(cells[...])
        gh[0:NODES, :] = high
        gl[0:NODES, :] = low
        face_out[...] = mm(fgat[...], gh[0:NODES, :]) + mm(fgat[...], gl[0:NODES, :])

        @pl.when(me > 0)
        def _():
            face_copy(step, True, me - 1).start()

        @pl.when(me < PARTS - 1)
        def _():
            face_copy(step, False, me + 1).start()

        collect(out1, in1, s1, r1)
        totals = mm(member[...], xh[...]) + mm(member[...], xl[...])
        high, low = split(totals)
        applied = mm(cbh[...], high) + (mm(cbh[...], low) + mm(cbl[...], high))
        high, low = split(applied)
        ph[0:TERMS, :] = high
        plo[0:TERMS, :] = low
        exchange(returned, out2, in2, s2, r2)

        @pl.when(me > 0)
        def _():
            face_wait(step, True, me - 1).wait()

        @pl.when(me < PARTS - 1)
        def _():
            face_wait(step, False, me + 1).wait()

        high, low = split(face_in[step])
        gh[0 : 2 * FACE, :] = high
        gl[0 : 2 * FACE, :] = low

        def assemble(i):
            at = rows_at(i)
            summed = cells[at, :] + mm(fsca[at, :], gh[0:256, :]) + mm(fsca[at, :], gl[0:256, :])
            field = filtered[at, :]
            cells[at, :] = (summed - centre * field) * gain - keep * previous[at, :]
            previous[at, :] = field

        loop(NODES // BLOCK, assemble)
        sent(out1, in1, s1, r1)
        collect(out2, in2, s2, r2)

        def finish(i):
            at = rows_at(i)
            back = mm(bth[at, :], xh[...]) + (mm(bth[at, :], xl[...]) + mm(btl[at, :], xh[...]))
            field = cells[at, :] + gain * back
            filtered[at, :] = field
            high, low = split(field)
            vh[at, :] = high
            vl[at, :] = low

        loop(NODES // BLOCK, finish)
        sent(out2, in2, s2, r2)

        @pl.when(step < 2)
        def _():
            exchange(coefficient, out1, in1, s1, r1)

    loop(3, degree)


def run_filter(scalars, bands_in, cell_ham, cell_nodes, left_face, right_face, proj_values, proj_nodes, slot_owner, slot_atom, coupling):
    owners = slot_owner[:, 0]
    ordinal = jnp.arange(SLOTS)
    position = jnp.sum((owners[:, None] == owners[None, :]) & (ordinal[None, :] < ordinal[:, None]), axis=1)
    bucket = owners * 2 + position
    placed = jnp.arange(2 * PARTS)[:, None] == bucket[None, :]
    slot = jnp.sum(jnp.where(placed, ordinal[None, :] + 1, 0), axis=1) - 1
    label = jnp.sum(jnp.where(placed, slot_atom[None, :] + 1, 0), axis=1) - 1
    slot, label = slot.reshape(PARTS, 2), label.reshape(PARTS, 2)
    lane = jnp.arange(128)
    labels = jnp.where(lane[None, :] < PROJ, label[:, :1], jnp.where(lane[None, :] < 40, label[:, 1:], -1))
    labels = jnp.broadcast_to(labels.astype(f32)[:, None, :], (PARTS, 8, 128))
    number = jnp.concatenate([jnp.arange(32), 32 + jnp.arange(8) % 4])
    taken = jnp.where(number[None, :] < PROJ, slot[:, :1], slot[:, 1:])
    source = jnp.where(taken < 0, -1, taken * PADDED + number[None, :] % PROJ)
    row_source = jnp.concatenate([source[:, :32].reshape(-1), source[:, 32:].reshape(-1)])[:, None]
    faces = jnp.concatenate([left_face, right_face], axis=1)
    padded = jnp.pad(coupling, ((0, 0), (0, PADDED - PROJ), (0, PADDED - PROJ))).reshape(TERMS, PADDED)
    vmem = pl.BlockSpec(memory_space=pltpu.VMEM)
    D = pltpu.SemaphoreType.DMA
    V = pltpu.VMEM
    return pl.pallas_call(
        filter_kernel,
        out_shape=jax.ShapeDtypeStruct((NODES, COLS), f32),
        in_specs=[pl.BlockSpec(memory_space=pltpu.SMEM)] + [vmem] * 11,
        out_specs=vmem,
        scratch_shapes=[
            V((SLOTS * PADDED, NODES), f32),
            V((SLOTS * PADDED, NODES), bf16),
            V((SLOTS * PADDED, NODES), bf16),
            V((ROWS, NODES), bf16),
            V((ROWS, NODES), bf16),
            V((NODES, ROWS), bf16),
            V((NODES, ROWS), bf16),
            V((CELLS * CELL, NODES), bf16),
            V((NODES, CELLS * CELL), bf16),
            V((2 * FACE, NODES), bf16),
            V((NODES, 2 * FACE), bf16),
            V((TERMS, ROWS), bf16),
            V((ROWS, TERMS), bf16),
            V((TERMS, TERMS), bf16),
            V((TERMS, TERMS), bf16),
            V((NODES, COLS), bf16),
            V((NODES, COLS), bf16),
            V((ROWS, COLS), bf16),
            V((ROWS, COLS), bf16),
            V((CELLS * CELL, COLS), bf16),
            V((CELLS * CELL, COLS), bf16),
            V((CELLS * CELL, COLS), bf16),
            V((CELLS * CELL, COLS), bf16),
            V((NODES, COLS), f32),
            V((NODES, COLS), f32),
            V((PARTS, 72, 128), f32),
            V((PARTS, 72, 128), f32),
            V((PARTS, 72, 128), f32),
            V((PARTS, 72, 128), f32),
            V((PARTS, 8, 128), f32),
            V((2 * FACE, COLS), f32),
            V((3, 2 * FACE, COLS), f32),
            D((PARTS,)),
            D((PARTS,)),
            D((PARTS,)),
            D((PARTS,)),
            D((PARTS,)),
            D((PARTS,)),
            D((2,)),
            D((3, 2)),
        ],
        compiler_params=pltpu.CompilerParams(
            collective_id=0, has_side_effects=True, vmem_limit_bytes=58 * 2**20
        ),
        name="filter_bands",
    )(
        scalars,
        bands_in,
        cell_ham,
        cell_nodes,
        cell_nodes.T,
        faces,
        faces.T,
        proj_values,
        proj_nodes.T,
        row_source.astype(i32),
        labels,
        padded,
    )


def passed_along(block, axis, distance):
    devices = range(lax.axis_size(axis))
    route = [((i - distance) % len(devices), i) for i in devices]
    return lax.ppermute(block, axis, route)


def cut_along(array, dim, count):
    lengths = array.shape
    parts = array.reshape(*lengths[:dim], count, lengths[dim] // count, *lengths[dim + 1 :])
    return jnp.moveaxis(parts, dim, 0)


def sum_at_owner(array, axis, dim):
    count = lax.axis_size(axis)
    parts = lax.all_to_all(cut_along(array, dim, count), axis, 0, 0, tiled=True)
    return jnp.sum(parts, axis=0)


def contract_rows(left_side, right_side):
    return lax.dot_general(left_side, right_side, (((0,), (0,)), ((), ())), precision=precise)


def per_device(
    bands_in,
    cell_ham,
    cell_nodes,
    left_face,
    right_face,
    proj_values,
    proj_nodes,
    slot_owner,
    slot_atom,
    coupling,
    node_weight,
    filter_center,
    filter_half,
):
    columns = bands_in.shape[1]
    scalars = jnp.stack([filter_center[0], filter_half[0]]).reshape(1, 2)
    filtered = run_filter(
        scalars, bands_in, cell_ham, cell_nodes, left_face, right_face, proj_values, proj_nodes, slot_owner, slot_atom, coupling
    )
    weighted = filtered * node_weight[:, None]
    groups = lax.axis_size("band")
    reach_count = groups // 2
    blocks = [contract_rows(weighted, filtered)]
    for offset in range(1, reach_count + 1):
        partner = passed_along(filtered, "band", -offset)
        blocks.append(contract_rows(weighted, partner))
    mirrored = []
    for offset in range(1, groups - reach_count):
        mirrored.append(passed_along(blocks[offset].T, "band", offset))
    blocks = blocks + mirrored[::-1]
    row_block = jnp.roll(jnp.concatenate(blocks, axis=1), lax.axis_index("band") * columns, axis=1)
    margin = sum_at_owner(row_block, "mesh", 1)
    return (filtered, margin)


def solution(mesh):
    placed = (
        P("mesh", "band"),
        P("mesh", None, None),
        P("mesh", None),
        P("mesh", None),
        P("mesh", None),
        P("mesh", None, None),
        P("mesh", None),
        P("mesh", None),
        P("mesh"),
        P("mesh", None, None),
        P("mesh"),
        P(),
        P(),
    )
    return jax.shard_map(
        per_device,
        mesh=mesh,
        in_specs=placed,
        out_specs=(P("mesh", "band"), P("band", "mesh")),
        check_vma=False,
    )
```

```python
import jax
import jax.numpy as jnp
from jax import lax
from jax.experimental import pallas as pl
from jax.experimental.pallas import tpu as pltpu
from jax.sharding import PartitionSpec as P

MESH = pl.DeviceIdType.MESH
f32, bf16, i32 = jnp.float32, jnp.bfloat16, jnp.int32

PARTS = 32
NODES = 1024
COLS = 256
SLOTS = 32
PROJ = 18
PADDED = 24
ATOMS = 16
CELLS = 3
CELL = 512
FACE = 128
MAIN = PARTS * 32
ROWS = MAIN + PARTS * 8
TERMS = ATOMS * PADDED
BLOCK = 256
GROUPS = 8


def mm(a, b):
    return jnp.dot(a, b, preferred_element_type=f32)


def split(x):
    high = x.astype(bf16)
    return high, (x - high.astype(f32)).astype(bf16)


def iota(shape, dim):
    return lax.broadcasted_iota(i32, shape, dim)


def hot(mask):
    return jnp.where(mask, 1.0, 0.0).astype(bf16)


def rows_at(index, size=BLOCK):
    return pl.ds(pl.multiple_of(index * size, size), size)


def loop(count, body):
    def step(i, carry):
        body(i)
        return carry

    lax.fori_loop(0, count, step, 0)


def filter_kernel(
    scalars,
    bands_in,
    cell_ham,
    cell_rows,
    cell_cols,
    face_row,
    face_col,
    proj_values,
    proj_cols,
    row_source,
    labels,
    coupling,
    node_weight,
    filtered,
    margin,
    b24,
    b24h,
    b24l,
    b8h,
    b8l,
    bth,
    btl,
    gat,
    sca,
    fgat,
    fsca,
    member,
    memt,
    cbh,
    cbl,
    vh,
    vl,
    xh,
    xl,
    gh,
    gl,
    ph,
    plo,
    cells,
    previous,
    out1,
    in1,
    out2,
    in2,
    lab_in,
    face_out,
    face_in,
    s1,
    r1,
    s2,
    r2,
    sl,
    rl,
    sf,
    rf,
    wth,
    wtl,
    halves,
    kept,
    given,
    core_in,
    strips,
    turned,
    swapped,
    sh,
    rh,
    sc,
    rc,
    ss,
    rs,
    sw,
    rw,
):
    me = lax.axis_index("mesh")
    band = lax.axis_index("band")
    other = me // 4
    quarter = lax.rem(me, 4)
    centre, half = scalars[0, 0], scalars[0, 1]

    def peer(k):
        return lax.rem(me + k, PARTS)

    face_in[...] = jnp.zeros_like(face_in)
    barrier = pltpu.get_barrier_semaphore()

    def greet(k):
        pl.semaphore_signal(barrier, inc=1, device_id=(band, peer(k + 1)), device_id_type=MESH)

    loop(PARTS - 1, greet)

    def greet_group(k):
        group = lax.rem(band + k + 1, GROUPS)
        pl.semaphore_signal(barrier, inc=1, device_id=(group, me), device_id_type=MESH)

    loop(GROUPS - 1, greet_group)

    @pl.when(other != band)
    def _():
        def greet_mirror(j):
            pl.semaphore_signal(barrier, inc=1, device_id=(other, band * 4 + j), device_id_type=MESH)

        loop(4, greet_mirror)

    b24[...] = jnp.zeros_like(b24)
    for s in range(SLOTS):
        spread = hot(proj_cols[:, s : s + 1] == iota((128, NODES), 1))
        high, low = split(proj_values[s])
        b24[s * PADDED : s * PADDED + PROJ, :] = mm(high, spread) + mm(low, spread)
    high, low = split(b24[...])
    b24h[...] = high
    b24l[...] = low

    def place(i):
        at = rows_at(i)
        chosen = hot(row_source[at, :] == iota((BLOCK, SLOTS * PADDED), 1))
        b8h[at, :] = mm(chosen, b24h[...]).astype(bf16)
        b8l[at, :] = mm(chosen, b24l[...]).astype(bf16)

    loop(ROWS // BLOCK, place)

    def set_field(x):
        high, low = split(x)
        vh[...] = high
        vl[...] = low

    filtered[...] = bands_in[...]
    previous[...] = bands_in[...]
    set_field(bands_in[...])

    def copy_to(source, target, send, receive, o):
        return pltpu.make_async_remote_copy(
            source.at[o],
            target.at[me],
            send.at[o],
            receive.at[me],
            device_id=(band, o),
            device_id_type=MESH,
        )

    def arrival(source, target, send, receive, q):
        return pltpu.make_async_remote_copy(
            source.at[q],
            target.at[q],
            send.at[q],
            receive.at[q],
            device_id=(band, q),
            device_id_type=MESH,
        )

    def exchange(rows_of, out, target, send, receive, wait=None):
        tail = rows_of(MAIN // BLOCK)
        first = lax.rem(iota((BLOCK, 128), 0), 8) < 4
        out[:, 64:72, :] = jnp.where(first, tail[:, :128], tail[:, 128:]).reshape(PARTS, 8, 128)

        def group(t):
            g = lax.rem(me // 8 + 1 + t, 4)
            block = rows_of(g)
            out[pl.ds(g * 8, 8), 0:32, :] = block[:, :128].reshape(8, 32, 128)
            out[pl.ds(g * 8, 8), 32:64, :] = block[:, 128:].reshape(8, 32, 128)

            def one(i):
                o = g * 8 + lax.rem(me + i, 8)

                @pl.when(o != me)
                def _():
                    copy_to(out, target, send, receive, o).start()

            loop(8, one)

        loop(4, group)
        target[me] = out[me]

    def collect(out, target, send, receive):
        def one(k):
            arrival(out, target, send, receive, peer(k + 1)).wait_recv()

        loop(PARTS - 1, one)
        main = target[:, 0:64, :]
        left = main[:, 0:32, :].reshape(MAIN, 128)
        right = main[:, 32:64, :].reshape(MAIN, 128)
        tail = target[:, 64:72, :].reshape(BLOCK, 128)
        first = lax.rem(iota((BLOCK, 128), 0), 8) < 4
        for columns, top, keep in ((0, left, first), (128, right, jnp.logical_not(first))):
            high, low = split(top)
            xh[0:MAIN, columns : columns + 128] = high
            xl[0:MAIN, columns : columns + 128] = low
            high, low = split(jnp.where(keep, tail, 0.0))
            xh[MAIN:ROWS, columns : columns + 128] = high
            xl[MAIN:ROWS, columns : columns + 128] = low

    def sent(out, target, send, receive):
        def one(k):
            arrival(out, target, send, receive, peer(k + 1)).wait_send()

        loop(PARTS - 1, one)

    def coefficient(i):
        at = rows_at(i)
        return mm(b8h[at, :], vh[...]) + (mm(b8h[at, :], vl[...]) + mm(b8l[at, :], vh[...]))

    pl.semaphore_wait(barrier, jnp.where(other != band, 4, 0) + PARTS - 1 + GROUPS - 1)

    def tell(k):
        copy_to(labels, lab_in, sl, rl, peer(k + 1)).start()

    loop(PARTS - 1, tell)
    exchange(coefficient, out1, in1, s1, r1)
    lab_in[me] = labels[me]

    for c in range(CELLS):
        for h in range(2):
            gat[c * CELL + h * BLOCK : c * CELL + (h + 1) * BLOCK, :] = hot(
                cell_cols[h * BLOCK : (h + 1) * BLOCK, c : c + 1] == iota((BLOCK, NODES), 1)
            )
    for i in range(NODES // BLOCK):
        row = iota((BLOCK, CELL), 0) + i * BLOCK
        for c in range(CELLS):
            sca[i * BLOCK : (i + 1) * BLOCK, c * CELL : (c + 1) * CELL] = hot(row == cell_rows[c : c + 1, :])
        fsca[i * BLOCK : (i + 1) * BLOCK, :] = hot(row[:, :256] == face_row[...])
    fgat[...] = hot(face_col[...] == iota((2 * FACE, NODES), 1))
    for i in range(ROWS // BLOCK):
        at = slice(i * BLOCK, (i + 1) * BLOCK)
        bth[:, at] = b8h[at, :].astype(f32).T.astype(bf16)
        btl[:, at] = b8l[at, :].astype(f32).T.astype(bf16)
    repeat = hot(iota((PADDED, TERMS), 0) == lax.rem(iota((PADDED, TERMS), 1), PADDED))
    same = iota((TERMS, TERMS), 0) // PADDED == iota((TERMS, TERMS), 1) // PADDED
    high, low = split(coupling[...])
    cbh[...] = jnp.where(same, mm(high, repeat), 0.0).astype(bf16)
    cbl[...] = jnp.where(same, mm(low, repeat), 0.0).astype(bf16)

    def told(k):
        arrival(labels, lab_in, sl, rl, peer(k + 1)).wait()

    loop(PARTS - 1, told)
    col = iota((128, ROWS), 1)
    index = jnp.where(col < MAIN, lax.rem(col, 32), 32 + lax.rem(col, 8))
    place_of = hot(iota((128, ROWS), 0) == index)
    named = mm(lab_in[...].reshape(PARTS * 8, 128).astype(bf16), place_of)
    col = iota((PARTS * 8, ROWS), 1)
    source = jnp.where(col < MAIN, col // 32, (col - MAIN) // 8)
    atom = jnp.sum(jnp.where(iota((PARTS * 8, ROWS), 0) == source * 8, named, 0.0), axis=0, keepdims=True)
    col = iota((1, ROWS), 1)
    number = jnp.where(col < MAIN, lax.rem(col, 32), 32 + lax.rem(col, 4))
    key = jnp.where(atom < 0.0, -1, atom.astype(i32) * PADDED + lax.rem(number, PROJ))
    for i in range(ROWS // BLOCK):
        at = slice(i * BLOCK, (i + 1) * BLOCK)
        mask = jnp.where(iota((TERMS, BLOCK), 0) == key[:, at], 1.0, 0.0)
        member[:, at] = mask.astype(bf16)
        memt[at, :] = mask.T.astype(bf16)

    def returned(i):
        at = rows_at(i)
        return mm(memt[at, :], ph[0:TERMS, :]) + mm(memt[at, :], plo[0:TERMS, :])

    def face_copy(step, low, other):
        source = face_out.at[pl.ds(0 if low else FACE, FACE)]
        target = face_in.at[step, pl.ds(FACE if low else 0, FACE)]
        side = 0 if low else 1
        return pltpu.make_async_remote_copy(
            source, target, sf.at[side], rf.at[step, 1 - side], device_id=(band, other), device_id_type=MESH
        )

    def face_wait(step, low, other):
        source = face_out.at[pl.ds(0 if low else FACE, FACE)]
        target = face_in.at[step, pl.ds(0 if low else FACE, FACE)]
        side = 0 if low else 1
        return pltpu.make_async_remote_copy(
            source, target, sf.at[side], rf.at[step, side], device_id=(band, other), device_id_type=MESH
        )

    def degree(step):
        gain = jnp.where(step == 0, 1.0, 2.0) / half
        keep = jnp.where(step == 0, 0.0, 1.0)

        def pick(i):
            at = rows_at(i)
            gh[at, :] = mm(gat[at, :], vh[...]).astype(bf16)
            gl[at, :] = mm(gat[at, :], vl[...]).astype(bf16)

        loop(CELLS * CELL // BLOCK, pick)

        def multiply(c):
            at = rows_at(c, CELL)
            for h in range(2):
                high, low = split(cell_ham[c, h * BLOCK : (h + 1) * BLOCK, :])
                result = mm(high, gh[at, :]) + (mm(high, gl[at, :]) + mm(low, gh[at, :]))
                high, low = split(result)
                to = pl.ds(pl.multiple_of(c * CELL + h * BLOCK, BLOCK), BLOCK)
                ph[to, :] = high
                plo[to, :] = low

        loop(CELLS, multiply)

        def add(i):
            at = rows_at(i)
            cells[at, :] = mm(sca[at, :], ph[...]) + mm(sca[at, :], plo[...])

        loop(NODES // BLOCK, add)
        high, low = split(cells[...])
        gh[0:NODES, :] = high
        gl[0:NODES, :] = low
        face_out[...] = mm(fgat[...], gh[0:NODES, :]) + mm(fgat[...], gl[0:NODES, :])

        @pl.when(me > 0)
        def _():
            face_copy(step, True, me - 1).start()

        @pl.when(me < PARTS - 1)
        def _():
            face_copy(step, False, me + 1).start()

        collect(out1, in1, s1, r1)
        totals = mm(member[...], xh[...]) + mm(member[...], xl[...])
        high, low = split(totals)
        applied = mm(cbh[...], high) + (mm(cbh[...], low) + mm(cbl[...], high))
        high, low = split(applied)
        ph[0:TERMS, :] = high
        plo[0:TERMS, :] = low
        exchange(returned, out2, in2, s2, r2)

        @pl.when(me > 0)
        def _():
            face_wait(step, True, me - 1).wait()

        @pl.when(me < PARTS - 1)
        def _():
            face_wait(step, False, me + 1).wait()

        high, low = split(face_in[step])
        gh[0 : 2 * FACE, :] = high
        gl[0 : 2 * FACE, :] = low

        def assemble(i):
            at = rows_at(i)
            summed = cells[at, :] + mm(fsca[at, :], gh[0:256, :]) + mm(fsca[at, :], gl[0:256, :])
            field = filtered[at, :]
            cells[at, :] = (summed - centre * field) * gain - keep * previous[at, :]
            previous[at, :] = field

        loop(NODES // BLOCK, assemble)
        sent(out1, in1, s1, r1)
        collect(out2, in2, s2, r2)

        def finish(i):
            at = rows_at(i)
            back = mm(bth[at, :], xh[...]) + (mm(bth[at, :], xl[...]) + mm(btl[at, :], xh[...]))
            field = cells[at, :] + gain * back
            filtered[at, :] = field
            high, low = split(field)
            vh[at, :] = high
            vl[at, :] = low

        loop(NODES // BLOCK, finish)
        sent(out2, in2, s2, r2)

        @pl.when(step < 2)
        def _():
            exchange(coefficient, out1, in1, s1, r1)

    loop(3, degree)
    margin_of(
        me, band, other, quarter, node_weight, filtered, margin, vh, vl, wth, wtl, halves, kept, given, core_in, strips,
        turned, swapped, sh, rh, sc, rc, ss, rs, sw, rw,
    )


def margin_of(
    me, band, other, quarter, node_weight, filtered, margin, vh, vl, wth, wtl, halves, kept, given, core_in, strips,
    turned, swapped, sh, rh, sc, rc, ss, rs, sw, rw,
):
    y, x = band // 2, lax.rem(band, 2)
    core, chip = lax.rem(me, 2), me // 2
    sibling = me + 1 - 2 * core
    steps = (
        (0, 1, x, 1 - x),
        (1, 0, 0, 0),
        (3, 0, 1, 1),
        (1, 1, 0, 0),
        (3, 1, 1, 1),
        (2, 0, y // 2, 1 - y // 2),
        (2, 1, y // 2, 1 - y // 2),
    )

    def group_at(dy, dx):
        return lax.rem(y + dy, 4) * 2 + lax.rem(x + dx, 2)

    def half_copy(i):
        dy, dx, mine, _ = steps[i]
        return pltpu.make_async_remote_copy(
            filtered.at[rows_at(mine, NODES // 2)],
            halves.at[i],
            sh.at[i],
            rh.at[i],
            device_id=(group_at(dy, dx), me),
            device_id_type=MESH,
        )

    def core_copy(i):
        return pltpu.make_async_remote_copy(
            given.at[i], core_in.at[i], sc.at[i], rc.at[i], device_id=(band, sibling), device_id_type=MESH
        )

    def strip_copy(i, j, target):
        return pltpu.make_async_remote_copy(
            kept.at[i, j], strips.at[chip], ss.at[i, j], rs.at[chip], device_id=(band, target), device_id_type=MESH
        )

    for i in range(7):
        half_copy(i).start()
    for i in range(NODES // BLOCK):
        at = slice(i * BLOCK, (i + 1) * BLOCK)
        high, low = split(filtered[at, :].T * node_weight[:, at])
        wth[:, at] = high
        wtl[:, at] = low
    lower = iota((128, 128), 1) < 64
    owners = [band] + [group_at((4 - dy) % 4, dx) for dy, dx, _, _ in steps]

    def send_strips(i):
        core_copy(i).wait_recv()
        for j in range(2):
            kept[i, j] = kept[i, j] + core_in[i, j]
            target = owners[i] * 4 + 2 * j + core

            @pl.when(target == me)
            def _():
                strips[chip] = kept[i, j]

            @pl.when(target != me)
            def _():
                strip_copy(i, j, target).start()

    for i in range(GROUPS):
        if i == 0:
            product = mm(wth[...], vh[...]) + (mm(wth[...], vl[...]) + mm(wtl[...], vh[...]))
        else:
            half_copy(i - 1).wait_recv()
            at = rows_at(steps[i - 1][3], NODES // 2)
            high, low = split(halves[i - 1])
            product = mm(wth[:, at], high) + (mm(wth[:, at], low) + mm(wtl[:, at], high))
        for j in range(2):
            top, bottom = product[:128, j * 128 : (j + 1) * 128], product[128:, j * 128 : (j + 1) * 128]
            even = jnp.where(lower, top, pltpu.roll(bottom, 64, 1))
            odd = jnp.where(lower, pltpu.roll(top, 64, 1), bottom)
            kept[i, j] = jnp.where(core == 0, even, odd)
            given[i, j] = jnp.where(core == 0, odd, even)
        core_copy(i).start()
        if i > 0:
            send_strips(i - 1)
    send_strips(GROUPS - 1)

    def arrived(k):
        source = lax.rem(chip + k + 1, PARTS // 2)
        pltpu.make_async_remote_copy(
            kept.at[0, 0], strips.at[source], ss.at[0, 0], rs.at[source], device_id=(band, source * 2 + core), device_id_type=MESH
        ).wait_recv()

    loop(PARTS // 2 - 1, arrived)
    total = jnp.sum(strips[...], axis=0)
    margin[0:128, :] = total[:, :64]
    margin[128:256, :] = total[:, 64:]

    def swap_copy(j):
        return pltpu.make_async_remote_copy(
            turned.at[pl.ds(64 * (j // 2), 64)],
            swapped.at[quarter],
            sw.at[j],
            rw.at[quarter],
            device_id=(other, band * 4 + j),
            device_id_type=MESH,
        )

    @pl.when(other != band)
    def _():
        turned[...] = total.T
        for j in range(4):
            swap_copy(j).start()
        for j in range(4):
            pltpu.make_async_remote_copy(
                turned.at[pl.ds(0, 64)], swapped.at[j], sw.at[j], rw.at[j], device_id=(other, band * 4 + j), device_id_type=MESH
            ).wait_recv()
            tile = jnp.where(lax.rem(quarter, 2) == 0, swapped[j][:, :64], swapped[j][:, 64:])
            margin[j * 64 : (j + 1) * 64, :] += tile
        for j in range(4):
            swap_copy(j).wait_send()

    for i in range(7):
        half_copy(i).wait_send()
    for i in range(GROUPS):
        core_copy(i).wait_send()
        for j in range(2):
            target = owners[i] * 4 + 2 * j + core

            @pl.when(target != me)
            def _():
                strip_copy(i, j, target).wait_send()


def run_filter(scalars, bands_in, cell_ham, cell_nodes, left_face, right_face, proj_values, proj_nodes, slot_owner, slot_atom, coupling, node_weight):
    owners = slot_owner[:, 0]
    ordinal = jnp.arange(SLOTS)
    position = jnp.sum((owners[:, None] == owners[None, :]) & (ordinal[None, :] < ordinal[:, None]), axis=1)
    bucket = owners * 2 + position
    placed = jnp.arange(2 * PARTS)[:, None] == bucket[None, :]
    slot = jnp.sum(jnp.where(placed, ordinal[None, :] + 1, 0), axis=1) - 1
    label = jnp.sum(jnp.where(placed, slot_atom[None, :] + 1, 0), axis=1) - 1
    slot, label = slot.reshape(PARTS, 2), label.reshape(PARTS, 2)
    lane = jnp.arange(128)
    labels = jnp.where(lane[None, :] < PROJ, label[:, :1], jnp.where(lane[None, :] < 40, label[:, 1:], -1))
    labels = jnp.broadcast_to(labels.astype(f32)[:, None, :], (PARTS, 8, 128))
    number = jnp.concatenate([jnp.arange(32), 32 + jnp.arange(8) % 4])
    taken = jnp.where(number[None, :] < PROJ, slot[:, :1], slot[:, 1:])
    source = jnp.where(taken < 0, -1, taken * PADDED + number[None, :] % PROJ)
    row_source = jnp.concatenate([source[:, :32].reshape(-1), source[:, 32:].reshape(-1)])[:, None]
    faces = jnp.concatenate([left_face, right_face], axis=1)
    padded = jnp.pad(coupling, ((0, 0), (0, PADDED - PROJ), (0, PADDED - PROJ))).reshape(TERMS, PADDED)
    vmem = pl.BlockSpec(memory_space=pltpu.VMEM)
    D = pltpu.SemaphoreType.DMA
    V = pltpu.VMEM
    return pl.pallas_call(
        filter_kernel,
        out_shape=(jax.ShapeDtypeStruct((NODES, COLS), f32), jax.ShapeDtypeStruct((COLS, 64), f32)),
        in_specs=[pl.BlockSpec(memory_space=pltpu.SMEM)] + [vmem] * 12,
        out_specs=(vmem, vmem),
        scratch_shapes=[
            V((SLOTS * PADDED, NODES), f32),
            V((SLOTS * PADDED, NODES), bf16),
            V((SLOTS * PADDED, NODES), bf16),
            V((ROWS, NODES), bf16),
            V((ROWS, NODES), bf16),
            V((NODES, ROWS), bf16),
            V((NODES, ROWS), bf16),
            V((CELLS * CELL, NODES), bf16),
            V((NODES, CELLS * CELL), bf16),
            V((2 * FACE, NODES), bf16),
            V((NODES, 2 * FACE), bf16),
            V((TERMS, ROWS), bf16),
            V((ROWS, TERMS), bf16),
            V((TERMS, TERMS), bf16),
            V((TERMS, TERMS), bf16),
            V((NODES, COLS), bf16),
            V((NODES, COLS), bf16),
            V((ROWS, COLS), bf16),
            V((ROWS, COLS), bf16),
            V((CELLS * CELL, COLS), bf16),
            V((CELLS * CELL, COLS), bf16),
            V((CELLS * CELL, COLS), bf16),
            V((CELLS * CELL, COLS), bf16),
            V((NODES, COLS), f32),
            V((NODES, COLS), f32),
            V((PARTS, 72, 128), f32),
            V((PARTS, 72, 128), f32),
            V((PARTS, 72, 128), f32),
            V((PARTS, 72, 128), f32),
            V((PARTS, 8, 128), f32),
            V((2 * FACE, COLS), f32),
            V((3, 2 * FACE, COLS), f32),
            D((PARTS,)),
            D((PARTS,)),
            D((PARTS,)),
            D((PARTS,)),
            D((PARTS,)),
            D((PARTS,)),
            D((2,)),
            D((3, 2)),
            V((COLS, NODES), bf16),
            V((COLS, NODES), bf16),
            V((7, NODES // 2, COLS), f32),
            V((GROUPS, 2, 128, 128), f32),
            V((GROUPS, 2, 128, 128), f32),
            V((GROUPS, 2, 128, 128), f32),
            V((PARTS // 2, 128, 128), f32),
            V((128, 128), f32),
            V((4, 64, 128), f32),
            D((7,)),
            D((7,)),
            D((GROUPS,)),
            D((GROUPS,)),
            D((GROUPS, 2)),
            D((PARTS // 2,)),
            D((4,)),
            D((4,)),
        ],
        compiler_params=pltpu.CompilerParams(
            collective_id=0, has_side_effects=True, vmem_limit_bytes=58 * 2**20
        ),
        name="filter_bands",
    )(
        scalars,
        bands_in,
        cell_ham,
        cell_nodes,
        cell_nodes.T,
        faces,
        faces.T,
        proj_values,
        proj_nodes.T,
        row_source.astype(i32),
        labels,
        padded,
        node_weight[None, :],
    )


def per_device(
    bands_in,
    cell_ham,
    cell_nodes,
    left_face,
    right_face,
    proj_values,
    proj_nodes,
    slot_owner,
    slot_atom,
    coupling,
    node_weight,
    filter_center,
    filter_half,
):
    scalars = jnp.stack([filter_center[0], filter_half[0]]).reshape(1, 2)
    return run_filter(
        scalars, bands_in, cell_ham, cell_nodes, left_face, right_face, proj_values, proj_nodes, slot_owner, slot_atom, coupling,
        node_weight,
    )


def solution(mesh):
    placed = (
        P("mesh", "band"),
        P("mesh", None, None),
        P("mesh", None),
        P("mesh", None),
        P("mesh", None),
        P("mesh", None, None),
        P("mesh", None),
        P("mesh", None),
        P("mesh"),
        P("mesh", None, None),
        P("mesh"),
        P(),
        P(),
    )
    return jax.shard_map(
        per_device,
        mesh=mesh,
        in_specs=placed,
        out_specs=(P("mesh", "band"), P("band", "mesh")),
        check_vma=False,
    )
```

```python
import jax
import jax.numpy as jnp
from jax import lax
from jax.experimental import pallas as pl
from jax.experimental.pallas import tpu as pltpu
from jax.sharding import PartitionSpec as P

MESH = pl.DeviceIdType.MESH
f32, bf16, i32 = jnp.float32, jnp.bfloat16, jnp.int32

PARTS = 32
NODES = 1024
COLS = 256
SLOTS = 32
PROJ = 18
PADDED = 24
ATOMS = 16
CELLS = 3
CELL = 512
FACE = 128
WIDE = 40
ROWS = PARTS * WIDE
TERMS = ATOMS * PADDED
BLOCK = 256
GROUPS = 8


def mm(a, b):
    return jnp.dot(a, b, preferred_element_type=f32)


def split(x):
    high = x.astype(bf16)
    return high, (x - high.astype(f32)).astype(bf16)


def iota(shape, dim):
    return lax.broadcasted_iota(i32, shape, dim)


def hot(mask):
    return jnp.where(mask, 1.0, 0.0).astype(bf16)


def rows_at(index, size=BLOCK):
    return pl.ds(pl.multiple_of(index * size, size), size)


def loop(count, body):
    def step(i, carry):
        body(i)
        return carry

    lax.fori_loop(0, count, step, 0)


def filter_kernel(
    centre_ref,
    half_ref,
    bands_in,
    cell_ham,
    cell_nodes,
    left_face,
    right_face,
    proj_values,
    proj_nodes,
    slot_owner,
    slot_atom,
    coupling,
    node_weight,
    filtered,
    margin,
    stacked,
    coupled,
    b24,
    b24h,
    b24l,
    b24th,
    b24tl,
    place,
    placet,
    gat,
    sca,
    fgat,
    fsca,
    member,
    memt,
    cbh,
    cbl,
    vh,
    vl,
    xh,
    xl,
    gh,
    gl,
    ph,
    plo,
    cells,
    previous,
    out1,
    in1,
    out2,
    in2,
    labels,
    lab_in,
    face_out,
    face_in,
    s1,
    r1,
    s2,
    r2,
    sl,
    rl,
    sf,
    rf,
    wth,
    wtl,
    halves,
    kept,
    given,
    core_in,
    strips,
    turned,
    swapped,
    sh,
    rh,
    sc,
    rc,
    ss,
    rs,
    sw,
    rw,
):
    me = lax.axis_index("mesh")
    band = lax.axis_index("band")
    other = me // 4
    quarter = lax.rem(me, 4)
    centre, half = centre_ref[0], half_ref[0]

    def peer(k):
        return lax.rem(me + k, PARTS)

    face_in[...] = jnp.zeros_like(face_in)
    in1[...] = jnp.zeros_like(in1)
    in2[...] = jnp.zeros_like(in2)
    barrier = pltpu.get_barrier_semaphore()

    def greet(k):
        pl.semaphore_signal(barrier, inc=1, device_id=(band, peer(k + 1)), device_id_type=MESH)

    loop(PARTS - 1, greet)

    def greet_group(k):
        group = lax.rem(band + k + 1, GROUPS)
        pl.semaphore_signal(barrier, inc=1, device_id=(group, me), device_id_type=MESH)

    loop(GROUPS - 1, greet_group)

    @pl.when(other != band)
    def _():
        def greet_mirror(j):
            pl.semaphore_signal(barrier, inc=1, device_id=(other, band * 4 + j), device_id_type=MESH)

        loop(4, greet_mirror)

    stacked[...] = jnp.zeros_like(stacked)
    for s in range(SLOTS):
        stacked[s * PADDED : s * PADDED + PROJ, :] = proj_values[:, s, :]
    slot_cols = proj_nodes[...].astype(f32).T
    node = iota((128, NODES), 1).astype(f32)
    upper = lax.rem(iota((4 * PADDED, 128), 0), 2 * PADDED) < PADDED
    for t in range(SLOTS // 2):
        at = slice(t * 2 * PADDED, (t + 1) * 2 * PADDED)
        spread = jnp.concatenate([hot(slot_cols[:, s : s + 1] == node) for s in (2 * t, 2 * t + 1)], axis=0)
        values = stacked[at, :]
        high = values.astype(bf16).astype(f32)
        both = jnp.concatenate([high, values - high], axis=0)
        both = jnp.concatenate([jnp.where(upper, both, 0.0), jnp.where(upper, 0.0, both)], axis=1)
        result = mm(both.astype(bf16), spread)
        b24[at, :] = result[: 2 * PADDED] + result[2 * PADDED :]
    high, low = split(b24[...])
    b24h[...] = high
    b24l[...] = low

    owner_row = slot_owner[...].astype(f32)
    atom_row = slot_atom[...].astype(f32)
    down, across = iota((SLOTS, SLOTS), 0), iota((SLOTS, SLOTS), 1)
    owner_col = jnp.sum(jnp.where(down == across, owner_row, 0.0), axis=1, keepdims=True)
    earlier = jnp.where((owner_col == owner_row) & (across < down), 1.0, 0.0)
    bucket_col = 2.0 * owner_col + jnp.sum(earlier, axis=1, keepdims=True)
    bucket_row = jnp.sum(jnp.where(down == across, bucket_col, 0.0), axis=0, keepdims=True)
    shape = (SLOTS, SLOTS * PADDED)
    spot = jnp.sum(jnp.where(iota(shape, 0) == iota(shape, 1) // PADDED, bucket_col, 0.0), axis=0, keepdims=True)
    lane = lax.rem(iota((1, SLOTS * PADDED), 1), PADDED)
    spot = jnp.where(lane < PROJ, spot.astype(i32) * PADDED + lane, -2)
    shape = (SLOTS * PADDED, SLOTS)
    spot_col = jnp.sum(jnp.where(iota(shape, 1) == iota(shape, 0) // PADDED, bucket_row, 0.0), axis=1, keepdims=True)
    lane = lax.rem(iota((SLOTS * PADDED, 1), 0), PADDED)
    spot_col = jnp.where(lane < PROJ, spot_col.astype(i32) * PADDED + lane, -2)

    def row_key(row):
        number = lax.rem(row, WIDE)
        key = (2 * (row // WIDE) + number // PROJ) * PADDED + lax.rem(number, PROJ)
        return jnp.where(number < 2 * PROJ, key, -1)

    for i in range(ROWS // BLOCK):
        at = slice(i * BLOCK, (i + 1) * BLOCK)
        place[at, :] = hot(row_key(iota((BLOCK, 1), 0) + i * BLOCK) == spot)

    previous[...] = bands_in[...]
    filtered[...] = bands_in[...]
    high, low = split(bands_in[...])
    vh[...] = high
    vl[...] = low

    def sides(h):
        return slice(h * 128, (h + 1) * 128)

    def copy_to(source, target, send, receive, h, o):
        return pltpu.make_async_remote_copy(
            source.at[h, o, pl.ds(0, 2 * PROJ)],
            target.at[h, me, pl.ds(0, 2 * PROJ)],
            send.at[h, o],
            receive.at[h, me],
            device_id=(band, o),
            device_id_type=MESH,
        )

    def arrival(source, target, send, receive, h, q):
        return pltpu.make_async_remote_copy(
            source.at[h, q, pl.ds(0, 2 * PROJ)],
            target.at[h, q, pl.ds(0, 2 * PROJ)],
            send.at[h, q],
            receive.at[h, q],
            device_id=(band, q),
            device_id_type=MESH,
        )

    def exchange(h, rows_of, out, target, send, receive):
        def group(t):
            g = lax.rem(me // 16 + 1 + t, 2)
            out[h, pl.ds(g * 16, 16)] = rows_of(rows_at(g, ROWS // 2)).reshape(16, WIDE, 128)

            def one(i):
                o = g * 16 + lax.rem(me + i, 16)

                @pl.when(o != me)
                def _():
                    copy_to(out, target, send, receive, h, o).start()

            loop(16, one)

        loop(2, group)
        target[h, me] = out[h, me]

    def collect(h, out, target, send, receive):
        def one(k):
            arrival(out, target, send, receive, h, peer(k + 1)).wait_recv()

        loop(PARTS - 1, one)
        high, low = split(target[h].reshape(ROWS, 128))
        xh[...] = high
        xl[...] = low

    def sent(h, out, target, send, receive):
        def one(k):
            arrival(out, target, send, receive, h, peer(k + 1)).wait_send()

        loop(PARTS - 1, one)

    def send_coefficients(h):
        columns = sides(h)
        fh, fl = vh[:, columns], vl[:, columns]
        high, low = split(mm(b24h[...], fh) + (mm(b24h[...], fl) + mm(b24l[...], fh)))
        exchange(h, lambda at: mm(place[at, :], high) + mm(place[at, :], low), out1, in1, s1, r1)

    pl.semaphore_wait(barrier, jnp.where(other != band, 4, 0) + PARTS - 1 + GROUPS - 1)
    for h in range(2):
        send_coefficients(h)

    target = iota((PARTS, SLOTS), 0).astype(f32) * 2.0
    first = jnp.sum(jnp.where(bucket_row == target, atom_row + 1.0, 0.0), axis=1, keepdims=True) - 1.0
    second = jnp.sum(jnp.where(bucket_row == target + 1.0, atom_row + 1.0, 0.0), axis=1, keepdims=True) - 1.0
    lane = iota((PARTS, 128), 1)
    named = jnp.where(lane < PROJ, first, jnp.where(lane < 2 * PROJ, second, -1.0))
    for o in range(PARTS):
        labels[o] = jnp.broadcast_to(named[o : o + 1, :], (8, 128))

    def label_to(o):
        return pltpu.make_async_remote_copy(
            labels.at[o], lab_in.at[me], sl.at[o], rl.at[me], device_id=(band, o), device_id_type=MESH
        )

    def label_from(q):
        return pltpu.make_async_remote_copy(
            labels.at[q], lab_in.at[q], sl.at[q], rl.at[q], device_id=(band, q), device_id_type=MESH
        )

    def tell(k):
        label_to(peer(k + 1)).start()

    loop(PARTS - 1, tell)
    lab_in[me] = labels[me]

    for i in range(NODES // BLOCK):
        at = slice(i * BLOCK, (i + 1) * BLOCK)
        row = iota((BLOCK, CELL), 0) + i * BLOCK
        for c in range(CELLS):
            mask = jnp.where(row == cell_nodes[c : c + 1, :], 1.0, 0.0)
            sca[at, c * CELL : (c + 1) * CELL] = mask.astype(bf16)
            gat[c * CELL : (c + 1) * CELL, at] = mask.T.astype(bf16)
        for side, face in enumerate((left_face, right_face)):
            mask = jnp.where(row[:, :FACE] == face[...], 1.0, 0.0)
            fsca[at, side * FACE : (side + 1) * FACE] = mask.astype(bf16)
            fgat[side * FACE : (side + 1) * FACE, at] = mask.T.astype(bf16)
    for i in range(SLOTS * PADDED // BLOCK):
        at = slice(i * BLOCK, (i + 1) * BLOCK)
        high, low = split(b24[at, :].T)
        b24th[:, at] = high
        b24tl[:, at] = low
        placet[at, :] = hot(spot_col[at, :] == row_key(iota((1, ROWS), 1)))
    coupled[...] = jnp.zeros_like(coupled)
    for a in range(ATOMS):
        coupled[a * PADDED : a * PADDED + PROJ, 0:PROJ] = coupling[:, a, :]
    repeat = hot(iota((128, TERMS), 0) == lax.rem(iota((128, TERMS), 1), PADDED))
    same = iota((TERMS, TERMS), 0) // PADDED == iota((TERMS, TERMS), 1) // PADDED
    high, low = split(coupled[...])
    cbh[...] = jnp.where(same, mm(high, repeat), 0.0).astype(bf16)
    cbl[...] = jnp.where(same, mm(low, repeat), 0.0).astype(bf16)

    def told(k):
        label_from(peer(k + 1)).wait()

    loop(PARTS - 1, told)
    number = lax.rem(iota((128, ROWS), 1), WIDE)
    named = mm(lab_in[...].reshape(PARTS * 8, 128).astype(bf16), hot(iota((128, ROWS), 0) == number))
    source = iota((PARTS * 8, ROWS), 1) // WIDE
    atom = jnp.sum(jnp.where(iota((PARTS * 8, ROWS), 0) == source * 8, named, 0.0), axis=0, keepdims=True)
    number = lax.rem(iota((1, ROWS), 1), WIDE)
    key = jnp.where(atom < 0.0, -1, atom.astype(i32) * PADDED + lax.rem(number, PROJ))
    for i in range(ROWS // BLOCK):
        at = slice(i * BLOCK, (i + 1) * BLOCK)
        mask = jnp.where(iota((TERMS, BLOCK), 0) == key[:, at], 1.0, 0.0)
        member[:, at] = mask.astype(bf16)
        memt[at, :] = mask.T.astype(bf16)

    def face_copy(step, low, other):
        source = face_out.at[pl.ds(0 if low else FACE, FACE)]
        target = face_in.at[step, pl.ds(FACE if low else 0, FACE)]
        side = 0 if low else 1
        return pltpu.make_async_remote_copy(
            source, target, sf.at[side], rf.at[step, 1 - side], device_id=(band, other), device_id_type=MESH
        )

    def face_wait(step, low, other):
        source = face_out.at[pl.ds(0 if low else FACE, FACE)]
        target = face_in.at[step, pl.ds(0 if low else FACE, FACE)]
        side = 0 if low else 1
        return pltpu.make_async_remote_copy(
            source, target, sf.at[side], rf.at[step, side], device_id=(band, other), device_id_type=MESH
        )

    def degree(step):
        gain = jnp.where(step == 0, 1.0, 2.0) / half
        keep = jnp.where(step == 0, 0.0, 1.0)

        def pick(c):
            at = rows_at(c, CELL)
            gh[at, :] = mm(gat[at, :], vh[...]).astype(bf16)
            gl[at, :] = mm(gat[at, :], vl[...]).astype(bf16)
            high, low = split(cell_ham[c])
            high, low = split(mm(high, gh[at, :]) + (mm(high, gl[at, :]) + mm(low, gh[at, :])))
            ph[at, :] = high
            plo[at, :] = low

        loop(CELLS, pick)

        def add(i):
            at = rows_at(i, 512)
            cells[at, :] = mm(sca[at, :], ph[...]) + mm(sca[at, :], plo[...])

        loop(NODES // 512, add)
        high, low = split(cells[...])
        gh[0:NODES, :] = high
        gl[0:NODES, :] = low
        face_out[...] = mm(fgat[...], gh[0:NODES, :]) + mm(fgat[...], gl[0:NODES, :])

        @pl.when(me > 0)
        def _():
            face_copy(step, True, me - 1).start()

        @pl.when(me < PARTS - 1)
        def _():
            face_copy(step, False, me + 1).start()

        for h in range(2):
            collect(h, out1, in1, s1, r1)
            high, low = split(mm(member[...], xh[...]) + mm(member[...], xl[...]))
            applied = mm(cbh[...], high) + (mm(cbh[...], low) + mm(cbl[...], high))
            high, low = split(applied)

            @pl.when(step > 0)
            def _():
                sent(h, out2, in2, s2, r2)

            exchange(h, lambda at: mm(memt[at, :], high) + mm(memt[at, :], low), out2, in2, s2, r2)

        @pl.when(me > 0)
        def _():
            face_wait(step, True, me - 1).wait()

        @pl.when(me < PARTS - 1)
        def _():
            face_wait(step, False, me + 1).wait()

        high, low = split(face_in[step])
        gh[0 : 2 * FACE, :] = high
        gl[0 : 2 * FACE, :] = low

        def assemble(i):
            at = rows_at(i, 512)
            summed = cells[at, :] + mm(fsca[at, :], gh[0:256, :]) + mm(fsca[at, :], gl[0:256, :])
            field = filtered[at, :]
            cells[at, :] = (summed - centre * field) * gain - keep * previous[at, :]
            previous[at, :] = field

        loop(NODES // 512, assemble)
        for h in range(2):
            columns = sides(h)
            collect(h, out2, in2, s2, r2)
            bh, bl = split(mm(placet[...], xh[...]) + mm(placet[...], xl[...]))

            def finish(i):
                at = rows_at(i, 512)
                back = mm(b24th[at, :], bh) + (mm(b24th[at, :], bl) + mm(b24tl[at, :], bh))
                field = cells[at, columns] + gain * back
                filtered[at, columns] = field
                high, low = split(field)
                vh[at, columns] = high
                vl[at, columns] = low

            loop(NODES // 512, finish)
            sent(h, out1, in1, s1, r1)

            @pl.when(step < 2)
            def _():
                send_coefficients(h)

    loop(3, degree)
    for h in range(2):
        sent(h, out2, in2, s2, r2)
    margin_of(
        me, band, other, quarter, node_weight, filtered, margin, vh, vl, wth, wtl, halves, kept, given, core_in, strips,
        turned, swapped, sh, rh, sc, rc, ss, rs, sw, rw,
    )


def margin_of(
    me, band, other, quarter, node_weight, filtered, margin, vh, vl, wth, wtl, halves, kept, given, core_in, strips,
    turned, swapped, sh, rh, sc, rc, ss, rs, sw, rw,
):
    y, x = band // 2, lax.rem(band, 2)
    core, chip = lax.rem(me, 2), me // 2
    sibling = me + 1 - 2 * core
    steps = (
        (0, 1, x, 1 - x),
        (1, 0, 0, 0),
        (3, 0, 1, 1),
        (1, 1, 0, 0),
        (3, 1, 1, 1),
        (2, 0, y // 2, 1 - y // 2),
        (2, 1, y // 2, 1 - y // 2),
    )

    def group_at(dy, dx):
        return lax.rem(y + dy, 4) * 2 + lax.rem(x + dx, 2)

    def half_copy(i):
        dy, dx, mine, _ = steps[i]
        return pltpu.make_async_remote_copy(
            filtered.at[rows_at(mine, NODES // 2)],
            halves.at[i],
            sh.at[i],
            rh.at[i],
            device_id=(group_at(dy, dx), me),
            device_id_type=MESH,
        )

    def core_copy(i):
        return pltpu.make_async_remote_copy(
            given.at[i], core_in.at[i], sc.at[i], rc.at[i], device_id=(band, sibling), device_id_type=MESH
        )

    def strip_copy(i, j, target):
        return pltpu.make_async_remote_copy(
            kept.at[i, j], strips.at[chip], ss.at[i, j], rs.at[chip], device_id=(band, target), device_id_type=MESH
        )

    for i in range(7):
        half_copy(i).start()
    for i in range(NODES // BLOCK):
        at = slice(i * BLOCK, (i + 1) * BLOCK)
        high, low = split(filtered[at, :].T * node_weight[:, at])
        wth[:, at] = high
        wtl[:, at] = low
    lower = iota((128, 128), 1) < 64
    owners = [band] + [group_at((4 - dy) % 4, dx) for dy, dx, _, _ in steps]

    def send_strips(i):
        core_copy(i).wait_recv()
        for j in range(2):
            kept[i, j] = kept[i, j] + core_in[i, j]
            target = owners[i] * 4 + 2 * j + core

            @pl.when(target == me)
            def _():
                strips[chip] = kept[i, j]

            @pl.when(target != me)
            def _():
                strip_copy(i, j, target).start()

    for i in range(GROUPS):
        if i == 0:
            product = mm(wth[...], vh[...]) + (mm(wth[...], vl[...]) + mm(wtl[...], vh[...]))
        else:
            half_copy(i - 1).wait_recv()
            at = rows_at(steps[i - 1][3], NODES // 2)
            high, low = split(halves[i - 1])
            product = mm(wth[:, at], high) + (mm(wth[:, at], low) + mm(wtl[:, at], high))
        for j in range(2):
            top, bottom = product[:128, j * 128 : (j + 1) * 128], product[128:, j * 128 : (j + 1) * 128]
            even = jnp.where(lower, top, pltpu.roll(bottom, 64, 1))
            odd = jnp.where(lower, pltpu.roll(top, 64, 1), bottom)
            kept[i, j] = jnp.where(core == 0, even, odd)
            given[i, j] = jnp.where(core == 0, odd, even)
        core_copy(i).start()
        if i > 0:
            send_strips(i - 1)
    send_strips(GROUPS - 1)

    def arrived(k):
        source = lax.rem(chip + k + 1, PARTS // 2)
        pltpu.make_async_remote_copy(
            kept.at[0, 0], strips.at[source], ss.at[0, 0], rs.at[source], device_id=(band, source * 2 + core), device_id_type=MESH
        ).wait_recv()

    loop(PARTS // 2 - 1, arrived)
    total = jnp.sum(strips[...], axis=0)
    flipped = total.T
    margin[:, :128] = flipped[:64]
    margin[:, 128:] = flipped[64:]

    def swap_copy(j):
        return pltpu.make_async_remote_copy(
            turned.at[pl.ds(64 * (j % 2), 64)],
            swapped.at[quarter],
            sw.at[j],
            rw.at[quarter],
            device_id=(other, band * 4 + j),
            device_id_type=MESH,
        )

    @pl.when(other != band)
    def _():
        turned[...] = total
        for j in range(4):
            swap_copy(j).start()
        for j in range(4):
            pltpu.make_async_remote_copy(
                turned.at[pl.ds(0, 64)], swapped.at[j], sw.at[j], rw.at[j], device_id=(other, band * 4 + j), device_id_type=MESH
            ).wait_recv()
        lowest = iota((64, 128), 1) < 64
        for j in range(2):
            even, odd = swapped[2 * j], swapped[2 * j + 1]
            left = jnp.where(lowest, even, pltpu.roll(odd, 64, 1))
            right = jnp.where(lowest, pltpu.roll(even, 64, 1), odd)
            margin[:, j * 128 : (j + 1) * 128] += jnp.where(quarter < 2, left, right)
        for j in range(4):
            swap_copy(j).wait_send()

    for i in range(7):
        half_copy(i).wait_send()
    for i in range(GROUPS):
        core_copy(i).wait_send()
        for j in range(2):
            target = owners[i] * 4 + 2 * j + core

            @pl.when(target != me)
            def _():
                strip_copy(i, j, target).wait_send()


def run_filter(
    bands_in, cell_ham, cell_nodes, left_face, right_face, proj_values, proj_nodes, slot_owner, slot_atom, coupling, node_weight,
    filter_center, filter_half,
):
    vmem = pl.BlockSpec(memory_space=pltpu.VMEM)
    smem = pl.BlockSpec(memory_space=pltpu.SMEM)
    D = pltpu.SemaphoreType.DMA
    V = pltpu.VMEM
    slot_rows = SLOTS * PADDED
    pairs = D((2, PARTS))
    filtered, margin = pl.pallas_call(
        filter_kernel,
        out_shape=(jax.ShapeDtypeStruct((NODES, COLS), f32), jax.ShapeDtypeStruct((64, COLS), f32)),
        in_specs=[smem] * 2 + [vmem] * 11,
        out_specs=(vmem, vmem),
        scratch_shapes=[
            V((slot_rows, 128), f32),
            V((TERMS, 128), f32),
            V((slot_rows, NODES), f32),
            V((slot_rows, NODES), bf16),
            V((slot_rows, NODES), bf16),
            V((NODES, slot_rows), bf16),
            V((NODES, slot_rows), bf16),
            V((ROWS, slot_rows), bf16),
            V((slot_rows, ROWS), bf16),
            V((CELLS * CELL, NODES), bf16),
            V((NODES, CELLS * CELL), bf16),
            V((2 * FACE, NODES), bf16),
            V((NODES, 2 * FACE), bf16),
            V((TERMS, ROWS), bf16),
            V((ROWS, TERMS), bf16),
            V((TERMS, TERMS), bf16),
            V((TERMS, TERMS), bf16),
            V((NODES, COLS), bf16),
            V((NODES, COLS), bf16),
            V((ROWS, 128), bf16),
            V((ROWS, 128), bf16),
            V((CELLS * CELL, COLS), bf16),
            V((CELLS * CELL, COLS), bf16),
            V((CELLS * CELL, COLS), bf16),
            V((CELLS * CELL, COLS), bf16),
            V((NODES, COLS), f32),
            V((NODES, COLS), f32),
            V((2, PARTS, WIDE, 128), f32),
            V((2, PARTS, WIDE, 128), f32),
            V((2, PARTS, WIDE, 128), f32),
            V((2, PARTS, WIDE, 128), f32),
            V((PARTS, 8, 128), f32),
            V((PARTS, 8, 128), f32),
            V((2 * FACE, COLS), f32),
            V((3, 2 * FACE, COLS), f32),
            pairs,
            pairs,
            pairs,
            pairs,
            D((PARTS,)),
            D((PARTS,)),
            D((2,)),
            D((3, 2)),
            V((COLS, NODES), bf16),
            V((COLS, NODES), bf16),
            V((7, NODES // 2, COLS), f32),
            V((GROUPS, 2, 128, 128), f32),
            V((GROUPS, 2, 128, 128), f32),
            V((GROUPS, 2, 128, 128), f32),
            V((PARTS // 2, 128, 128), f32),
            V((128, 128), f32),
            V((4, 64, 128), f32),
            D((7,)),
            D((7,)),
            D((GROUPS,)),
            D((GROUPS,)),
            D((GROUPS, 2)),
            D((PARTS // 2,)),
            D((4,)),
            D((4,)),
        ],
        compiler_params=pltpu.CompilerParams(
            collective_id=0, has_side_effects=True, vmem_limit_bytes=58 * 2**20
        ),
        name="filter_bands",
    )(
        filter_center,
        filter_half,
        bands_in,
        cell_ham,
        cell_nodes,
        left_face,
        right_face,
        jnp.transpose(proj_values, (1, 0, 2)),
        proj_nodes,
        slot_owner.reshape(1, SLOTS),
        slot_atom.reshape(1, SLOTS),
        jnp.transpose(coupling, (1, 0, 2)),
        node_weight.reshape(1, NODES),
    )
    return filtered, margin.T


def per_device(
    bands_in,
    cell_ham,
    cell_nodes,
    left_face,
    right_face,
    proj_values,
    proj_nodes,
    slot_owner,
    slot_atom,
    coupling,
    node_weight,
    filter_center,
    filter_half,
):
    return run_filter(
        bands_in, cell_ham, cell_nodes, left_face, right_face, proj_values, proj_nodes, slot_owner, slot_atom, coupling,
        node_weight, filter_center, filter_half,
    )


def solution(mesh):
    placed = (
        P("mesh", "band"),
        P("mesh", None, None),
        P("mesh", None),
        P("mesh", None),
        P("mesh", None),
        P("mesh", None, None),
        P("mesh", None),
        P("mesh", None),
        P("mesh"),
        P("mesh", None, None),
        P("mesh"),
        P(),
        P(),
    )
    return jax.shard_map(
        per_device,
        mesh=mesh,
        in_specs=placed,
        out_specs=(P("mesh", "band"), P("band", "mesh")),
        check_vma=False,
    )
```

```python
import jax
import jax.numpy as jnp
from jax import lax
from jax.experimental import pallas as pl
from jax.experimental.pallas import tpu as pltpu
from jax.sharding import PartitionSpec as P

MESH = pl.DeviceIdType.MESH
f32, bf16, i32 = jnp.float32, jnp.bfloat16, jnp.int32

PARTS = 32
NODES = 1024
COLS = 256
SLOTS = 32
PROJ = 18
PADDED = 24
ATOMS = 16
CELLS = 3
CELL = 512
FACE = 128
WIDE = 40
ROWS = PARTS * WIDE
TERMS = ATOMS * PADDED
BLOCK = 256
GROUPS = 8


def mm(a, b):
    return jnp.dot(a, b, preferred_element_type=f32)


def split(x):
    high = x.astype(bf16)
    return high, (x - high.astype(f32)).astype(bf16)


def iota(shape, dim):
    return lax.broadcasted_iota(i32, shape, dim)


def hot(mask):
    return jnp.where(mask, 1.0, 0.0).astype(bf16)


def rows_at(index, size=BLOCK):
    return pl.ds(pl.multiple_of(index * size, size), size)


def loop(count, body):
    def step(i, carry):
        body(i)
        return carry

    lax.fori_loop(0, count, step, 0)


def filter_kernel(
    centre_ref,
    half_ref,
    bands_in,
    cell_ham,
    cell_nodes,
    left_face,
    right_face,
    proj_values,
    proj_nodes,
    slot_owner,
    slot_atom,
    coupling,
    node_weight,
    filtered,
    margin,
    stacked,
    coupled,
    b24,
    b24h,
    b24l,
    b24th,
    b24tl,
    place,
    placet,
    gat,
    sca,
    fgat,
    fsca,
    member,
    memt,
    cbh,
    cbl,
    vh,
    vl,
    xh,
    xl,
    gh,
    gl,
    ph,
    plo,
    cells,
    previous,
    out1,
    in1,
    out2,
    in2,
    labels,
    lab_in,
    face_out,
    face_in,
    s1,
    r1,
    s2,
    r2,
    sl,
    rl,
    sf,
    rf,
    wth,
    wtl,
    product,
    halves,
    kept,
    given,
    core_in,
    strips,
    turned,
    swapped,
    sh,
    rh,
    sc,
    rc,
    ss,
    rs,
    sw,
    rw,
):
    me = lax.axis_index("mesh")
    band = lax.axis_index("band")
    other = me // 4
    quarter = lax.rem(me, 4)
    centre, half = centre_ref[0], half_ref[0]

    def peer(k):
        return lax.rem(me + k, PARTS)

    face_in[...] = jnp.zeros_like(face_in)
    in1[...] = jnp.zeros_like(in1)
    in2[...] = jnp.zeros_like(in2)
    barrier = pltpu.get_barrier_semaphore()

    def greet(k):
        pl.semaphore_signal(barrier, inc=1, device_id=(band, peer(k + 1)), device_id_type=MESH)

    loop(PARTS - 1, greet)

    def greet_group(k):
        group = lax.rem(band + k + 1, GROUPS)
        pl.semaphore_signal(barrier, inc=1, device_id=(group, me), device_id_type=MESH)

    loop(GROUPS - 1, greet_group)

    @pl.when(other != band)
    def _():
        def greet_mirror(j):
            pl.semaphore_signal(barrier, inc=1, device_id=(other, band * 4 + j), device_id_type=MESH)

        loop(4, greet_mirror)

    stacked[...] = jnp.zeros_like(stacked)
    for s in range(SLOTS):
        stacked[s * PADDED : s * PADDED + PROJ, :] = proj_values[:, s, :]
    slot_cols = proj_nodes[...].astype(f32).T
    node = iota((128, NODES), 1).astype(f32)
    upper = lax.rem(iota((4 * PADDED, 128), 0), 2 * PADDED) < PADDED
    for t in range(SLOTS // 2):
        at = slice(t * 2 * PADDED, (t + 1) * 2 * PADDED)
        spread = jnp.concatenate([hot(slot_cols[:, s : s + 1] == node) for s in (2 * t, 2 * t + 1)], axis=0)
        values = stacked[at, :]
        high = values.astype(bf16).astype(f32)
        both = jnp.concatenate([high, values - high], axis=0)
        both = jnp.concatenate([jnp.where(upper, both, 0.0), jnp.where(upper, 0.0, both)], axis=1)
        result = mm(both.astype(bf16), spread)
        b24[at, :] = result[: 2 * PADDED] + result[2 * PADDED :]
    high, low = split(b24[...])
    b24h[...] = high
    b24l[...] = low

    owner_row = slot_owner[...].astype(f32)
    atom_row = slot_atom[...].astype(f32)
    down, across = iota((SLOTS, SLOTS), 0), iota((SLOTS, SLOTS), 1)
    owner_col = jnp.sum(jnp.where(down == across, owner_row, 0.0), axis=1, keepdims=True)
    earlier = jnp.where((owner_col == owner_row) & (across < down), 1.0, 0.0)
    bucket_col = 2.0 * owner_col + jnp.sum(earlier, axis=1, keepdims=True)
    bucket_row = jnp.sum(jnp.where(down == across, bucket_col, 0.0), axis=0, keepdims=True)
    shape = (SLOTS, SLOTS * PADDED)
    spot = jnp.sum(jnp.where(iota(shape, 0) == iota(shape, 1) // PADDED, bucket_col, 0.0), axis=0, keepdims=True)
    lane = lax.rem(iota((1, SLOTS * PADDED), 1), PADDED)
    spot = jnp.where(lane < PROJ, spot.astype(i32) * PADDED + lane, -2)
    shape = (SLOTS * PADDED, SLOTS)
    spot_col = jnp.sum(jnp.where(iota(shape, 1) == iota(shape, 0) // PADDED, bucket_row, 0.0), axis=1, keepdims=True)
    lane = lax.rem(iota((SLOTS * PADDED, 1), 0), PADDED)
    spot_col = jnp.where(lane < PROJ, spot_col.astype(i32) * PADDED + lane, -2)

    def row_key(row):
        number = lax.rem(row, WIDE)
        key = (2 * (row // WIDE) + number // PROJ) * PADDED + lax.rem(number, PROJ)
        return jnp.where(number < 2 * PROJ, key, -1)

    for i in range(ROWS // BLOCK):
        at = slice(i * BLOCK, (i + 1) * BLOCK)
        place[at, :] = hot(row_key(iota((BLOCK, 1), 0) + i * BLOCK) == spot)

    previous[...] = bands_in[...]
    filtered[...] = bands_in[...]
    high, low = split(bands_in[...])
    vh[...] = high
    vl[...] = low

    def sides(h):
        return slice(h * 128, (h + 1) * 128)

    def copy_to(source, target, send, receive, h, o):
        return pltpu.make_async_remote_copy(
            source.at[h, o, pl.ds(0, 2 * PROJ)],
            target.at[h, me, pl.ds(0, 2 * PROJ)],
            send.at[h, o],
            receive.at[h, me],
            device_id=(band, o),
            device_id_type=MESH,
        )

    def arrival(source, target, send, receive, h, q):
        return pltpu.make_async_remote_copy(
            source.at[h, q, pl.ds(0, 2 * PROJ)],
            target.at[h, q, pl.ds(0, 2 * PROJ)],
            send.at[h, q],
            receive.at[h, q],
            device_id=(band, q),
            device_id_type=MESH,
        )

    def exchange(h, rows_of, out, target, send, receive):
        def group(t):
            g = lax.rem(me // 16 + 1 + t, 2)
            out[h, pl.ds(g * 16, 16)] = rows_of(rows_at(g, ROWS // 2)).reshape(16, WIDE, 128)

            def one(i):
                o = g * 16 + lax.rem(me + i, 16)

                @pl.when(o != me)
                def _():
                    copy_to(out, target, send, receive, h, o).start()

            loop(16, one)

        loop(2, group)
        target[h, me] = out[h, me]

    def collect(h, out, target, send, receive):
        def one(k):
            arrival(out, target, send, receive, h, peer(k + 1)).wait_recv()

        loop(PARTS - 1, one)
        high, low = split(target[h].reshape(ROWS, 128))
        xh[...] = high
        xl[...] = low

    def sent(h, out, target, send, receive):
        def one(k):
            arrival(out, target, send, receive, h, peer(k + 1)).wait_send()

        loop(PARTS - 1, one)

    def send_coefficients(h):
        columns = sides(h)
        fh, fl = vh[:, columns], vl[:, columns]
        high, low = split(mm(b24h[...], fh) + (mm(b24h[...], fl) + mm(b24l[...], fh)))
        exchange(h, lambda at: mm(place[at, :], high) + mm(place[at, :], low), out1, in1, s1, r1)

    pl.semaphore_wait(barrier, jnp.where(other != band, 4, 0) + PARTS - 1 + GROUPS - 1)
    for h in range(2):
        send_coefficients(h)

    target = iota((PARTS, SLOTS), 0).astype(f32) * 2.0
    first = jnp.sum(jnp.where(bucket_row == target, atom_row + 1.0, 0.0), axis=1, keepdims=True) - 1.0
    second = jnp.sum(jnp.where(bucket_row == target + 1.0, atom_row + 1.0, 0.0), axis=1, keepdims=True) - 1.0
    lane = iota((PARTS, 128), 1)
    named = jnp.where(lane < PROJ, first, jnp.where(lane < 2 * PROJ, second, -1.0))
    for o in range(PARTS):
        labels[o] = jnp.broadcast_to(named[o : o + 1, :], (8, 128))

    def label_to(o):
        return pltpu.make_async_remote_copy(
            labels.at[o], lab_in.at[me], sl.at[o], rl.at[me], device_id=(band, o), device_id_type=MESH
        )

    def label_from(q):
        return pltpu.make_async_remote_copy(
            labels.at[q], lab_in.at[q], sl.at[q], rl.at[q], device_id=(band, q), device_id_type=MESH
        )

    def tell(k):
        label_to(peer(k + 1)).start()

    loop(PARTS - 1, tell)
    lab_in[me] = labels[me]

    for i in range(NODES // BLOCK):
        at = slice(i * BLOCK, (i + 1) * BLOCK)
        row = iota((BLOCK, CELL), 0) + i * BLOCK
        for c in range(CELLS):
            mask = jnp.where(row == cell_nodes[c : c + 1, :], 1.0, 0.0)
            sca[at, c * CELL : (c + 1) * CELL] = mask.astype(bf16)
            gat[c * CELL : (c + 1) * CELL, at] = mask.T.astype(bf16)
        for side, face in enumerate((left_face, right_face)):
            mask = jnp.where(row[:, :FACE] == face[...], 1.0, 0.0)
            fsca[at, side * FACE : (side + 1) * FACE] = mask.astype(bf16)
            fgat[side * FACE : (side + 1) * FACE, at] = mask.T.astype(bf16)
    for i in range(SLOTS * PADDED // BLOCK):
        at = slice(i * BLOCK, (i + 1) * BLOCK)
        high, low = split(b24[at, :].T)
        b24th[:, at] = high
        b24tl[:, at] = low
        placet[at, :] = hot(spot_col[at, :] == row_key(iota((1, ROWS), 1)))
    coupled[...] = jnp.zeros_like(coupled)
    for a in range(ATOMS):
        coupled[a * PADDED : a * PADDED + PROJ, 0:PROJ] = coupling[:, a, :]
    repeat = hot(iota((128, TERMS), 0) == lax.rem(iota((128, TERMS), 1), PADDED))
    same = iota((TERMS, TERMS), 0) // PADDED == iota((TERMS, TERMS), 1) // PADDED
    high, low = split(coupled[...])
    cbh[...] = jnp.where(same, mm(high, repeat), 0.0).astype(bf16)
    cbl[...] = jnp.where(same, mm(low, repeat), 0.0).astype(bf16)

    def told(k):
        label_from(peer(k + 1)).wait()

    loop(PARTS - 1, told)
    number = lax.rem(iota((128, ROWS), 1), WIDE)
    named = mm(lab_in[...].reshape(PARTS * 8, 128).astype(bf16), hot(iota((128, ROWS), 0) == number))
    source = iota((PARTS * 8, ROWS), 1) // WIDE
    atom = jnp.sum(jnp.where(iota((PARTS * 8, ROWS), 0) == source * 8, named, 0.0), axis=0, keepdims=True)
    number = lax.rem(iota((1, ROWS), 1), WIDE)
    key = jnp.where(atom < 0.0, -1, atom.astype(i32) * PADDED + lax.rem(number, PROJ))
    for i in range(ROWS // BLOCK):
        at = slice(i * BLOCK, (i + 1) * BLOCK)
        mask = jnp.where(iota((TERMS, BLOCK), 0) == key[:, at], 1.0, 0.0)
        member[:, at] = mask.astype(bf16)
        memt[at, :] = mask.T.astype(bf16)

    def face_copy(step, low, other):
        source = face_out.at[pl.ds(0 if low else FACE, FACE)]
        target = face_in.at[step, pl.ds(FACE if low else 0, FACE)]
        side = 0 if low else 1
        return pltpu.make_async_remote_copy(
            source, target, sf.at[side], rf.at[step, 1 - side], device_id=(band, other), device_id_type=MESH
        )

    def face_wait(step, low, other):
        source = face_out.at[pl.ds(0 if low else FACE, FACE)]
        target = face_in.at[step, pl.ds(0 if low else FACE, FACE)]
        side = 0 if low else 1
        return pltpu.make_async_remote_copy(
            source, target, sf.at[side], rf.at[step, side], device_id=(band, other), device_id_type=MESH
        )

    def degree(step):
        gain = jnp.where(step == 0, 1.0, 2.0) / half
        keep = jnp.where(step == 0, 0.0, 1.0)

        def pick(c):
            at = rows_at(c, CELL)
            gh[at, :] = mm(gat[at, :], vh[...]).astype(bf16)
            gl[at, :] = mm(gat[at, :], vl[...]).astype(bf16)
            high, low = split(cell_ham[c])
            high, low = split(mm(high, gh[at, :]) + (mm(high, gl[at, :]) + mm(low, gh[at, :])))
            ph[at, :] = high
            plo[at, :] = low

        loop(CELLS, pick)

        def add(i):
            at = rows_at(i, 512)
            cells[at, :] = mm(sca[at, :], ph[...]) + mm(sca[at, :], plo[...])

        loop(NODES // 512, add)
        high, low = split(cells[...])
        gh[0:NODES, :] = high
        gl[0:NODES, :] = low
        face_out[...] = mm(fgat[...], gh[0:NODES, :]) + mm(fgat[...], gl[0:NODES, :])

        @pl.when(me > 0)
        def _():
            face_copy(step, True, me - 1).start()

        @pl.when(me < PARTS - 1)
        def _():
            face_copy(step, False, me + 1).start()

        for h in range(2):
            collect(h, out1, in1, s1, r1)
            high, low = split(mm(member[...], xh[...]) + mm(member[...], xl[...]))
            applied = mm(cbh[...], high) + (mm(cbh[...], low) + mm(cbl[...], high))
            high, low = split(applied)

            @pl.when(step > 0)
            def _():
                sent(h, out2, in2, s2, r2)

            exchange(h, lambda at: mm(memt[at, :], high) + mm(memt[at, :], low), out2, in2, s2, r2)

        @pl.when(me > 0)
        def _():
            face_wait(step, True, me - 1).wait()

        @pl.when(me < PARTS - 1)
        def _():
            face_wait(step, False, me + 1).wait()

        high, low = split(face_in[step])
        gh[0 : 2 * FACE, :] = high
        gl[0 : 2 * FACE, :] = low

        def assemble(i):
            at = rows_at(i, 512)
            summed = cells[at, :] + mm(fsca[at, :], gh[0:256, :]) + mm(fsca[at, :], gl[0:256, :])
            field = filtered[at, :]
            cells[at, :] = (summed - centre * field) * gain - keep * previous[at, :]
            previous[at, :] = field

        loop(NODES // 512, assemble)
        for h in range(2):
            columns = sides(h)
            collect(h, out2, in2, s2, r2)
            bh, bl = split(mm(placet[...], xh[...]) + mm(placet[...], xl[...]))

            def finish(i):
                at = rows_at(i, 512)
                back = mm(b24th[at, :], bh) + (mm(b24th[at, :], bl) + mm(b24tl[at, :], bh))
                field = cells[at, columns] + gain * back
                filtered[at, columns] = field
                high, low = split(field)
                vh[at, columns] = high
                vl[at, columns] = low

            loop(NODES // 512, finish)
            sent(h, out1, in1, s1, r1)

            @pl.when(step < 2)
            def _():
                send_coefficients(h)

    loop(3, degree)
    for h in range(2):
        sent(h, out2, in2, s2, r2)
    margin_of(
        me, band, other, quarter, node_weight, filtered, margin, vh, vl, wth, wtl, product, halves, kept, given, core_in, strips,
        turned, swapped, sh, rh, sc, rc, ss, rs, sw, rw,
    )


def margin_of(
    me, band, other, quarter, node_weight, filtered, margin, vh, vl, wth, wtl, product, halves, kept, given, core_in, strips,
    turned, swapped, sh, rh, sc, rc, ss, rs, sw, rw,
):
    y, x = band // 2, lax.rem(band, 2)
    core, chip = lax.rem(me, 2), me // 2
    sibling = me + 1 - 2 * core
    far = y // 2

    def choose(i, values):
        result = values[0]
        for k in range(1, GROUPS):
            result = jnp.where(i == k, values[k], result)
        return result

    def block_at(t):
        return lax.rem(t + chip, GROUPS)

    def group_at(dy, dx):
        return lax.rem(y + dy, 4) * 2 + lax.rem(x + dx, 2)

    def apart(i):
        return choose(i, (0, 0, 1, 3, 1, 3, 2, 2)), choose(i, (0, 1, 0, 0, 1, 1, 0, 1))

    def owner(i):
        dy, dx = apart(i)
        return group_at(4 - dy, dx)

    def half_copy(i):
        mine = choose(i, (0, x, 0, 1, 0, 1, far, far))
        return pltpu.make_async_remote_copy(
            filtered.at[rows_at(mine, NODES // 2)],
            halves.at[i - 1],
            sh.at[i - 1],
            rh.at[i - 1],
            device_id=(group_at(*apart(i)), me),
            device_id_type=MESH,
        )

    def core_copy(i):
        return pltpu.make_async_remote_copy(
            given.at[i], core_in.at[i], sc.at[i], rc.at[i], device_id=(band, sibling), device_id_type=MESH
        )

    def strip_copy(i, j, target):
        return pltpu.make_async_remote_copy(
            kept.at[i, j], strips.at[chip], ss.at[i, j], rs.at[chip], device_id=(band, target), device_id_type=MESH
        )

    def begin(t):
        i = block_at(t)

        @pl.when(i > 0)
        def _():
            half_copy(i).start()

    loop(GROUPS, begin)
    for i in range(NODES // BLOCK):
        at = slice(i * BLOCK, (i + 1) * BLOCK)
        high, low = split(filtered[at, :].T * node_weight[:, at])
        wth[:, at] = high
        wtl[:, at] = low
    lower = iota((128, 128), 1) < 64

    def send_strips(i):
        core_copy(i).wait_recv()
        for j in range(2):
            kept[i, j] = kept[i, j] + core_in[i, j]
            target = owner(i) * 4 + 2 * j + core

            @pl.when(target == me)
            def _():
                strips[chip] = kept[i, j]

            @pl.when(target != me)
            def _():
                strip_copy(i, j, target).start()

    def multiply(t):
        i = block_at(t)

        @pl.when(i == 0)
        def _():
            product[...] = mm(wth[...], vh[...]) + (mm(wth[...], vl[...]) + mm(wtl[...], vh[...]))

        @pl.when(i > 0)
        def _():
            half_copy(i).wait_recv()
            at = rows_at(choose(i, (0, 1 - x, 0, 1, 0, 1, 1 - far, 1 - far)), NODES // 2)
            high, low = split(halves[i - 1])
            product[...] = mm(wth[:, at], high) + (mm(wth[:, at], low) + mm(wtl[:, at], high))

        for j in range(2):
            top, bottom = product[:128, j * 128 : (j + 1) * 128], product[128:, j * 128 : (j + 1) * 128]
            even = jnp.where(lower, top, pltpu.roll(bottom, 64, 1))
            odd = jnp.where(lower, pltpu.roll(top, 64, 1), bottom)
            kept[i, j] = jnp.where(core == 0, even, odd)
            given[i, j] = jnp.where(core == 0, odd, even)
        core_copy(i).start()

        @pl.when(t > 0)
        def _():
            send_strips(block_at(t + GROUPS - 1))

    loop(GROUPS, multiply)
    send_strips(block_at(GROUPS - 1))

    def arrived(k):
        source = lax.rem(chip + k + 1, PARTS // 2)
        pltpu.make_async_remote_copy(
            kept.at[0, 0], strips.at[source], ss.at[0, 0], rs.at[source], device_id=(band, source * 2 + core), device_id_type=MESH
        ).wait_recv()

    loop(PARTS // 2 - 1, arrived)
    total = jnp.sum(strips[...], axis=0)
    flipped = total.T
    margin[:, :128] = flipped[:64]
    margin[:, 128:] = flipped[64:]

    def swap_copy(j):
        return pltpu.make_async_remote_copy(
            turned.at[pl.ds(64 * (j % 2), 64)],
            swapped.at[quarter],
            sw.at[j],
            rw.at[quarter],
            device_id=(other, band * 4 + j),
            device_id_type=MESH,
        )

    @pl.when(other != band)
    def _():
        turned[...] = total
        for j in range(4):
            swap_copy(j).start()
        for j in range(4):
            pltpu.make_async_remote_copy(
                turned.at[pl.ds(0, 64)], swapped.at[j], sw.at[j], rw.at[j], device_id=(other, band * 4 + j), device_id_type=MESH
            ).wait_recv()
        lowest = iota((64, 128), 1) < 64
        for j in range(2):
            even, odd = swapped[2 * j], swapped[2 * j + 1]
            left = jnp.where(lowest, even, pltpu.roll(odd, 64, 1))
            right = jnp.where(lowest, pltpu.roll(even, 64, 1), odd)
            margin[:, j * 128 : (j + 1) * 128] += jnp.where(quarter < 2, left, right)
        for j in range(4):
            swap_copy(j).wait_send()

    def finished(i):
        @pl.when(i > 0)
        def _():
            half_copy(i).wait_send()

        core_copy(i).wait_send()
        for j in range(2):
            target = owner(i) * 4 + 2 * j + core

            @pl.when(target != me)
            def _():
                strip_copy(i, j, target).wait_send()

    loop(GROUPS, finished)


def run_filter(
    bands_in, cell_ham, cell_nodes, left_face, right_face, proj_values, proj_nodes, slot_owner, slot_atom, coupling, node_weight,
    filter_center, filter_half,
):
    vmem = pl.BlockSpec(memory_space=pltpu.VMEM)
    smem = pl.BlockSpec(memory_space=pltpu.SMEM)
    D = pltpu.SemaphoreType.DMA
    V = pltpu.VMEM
    slot_rows = SLOTS * PADDED
    pairs = D((2, PARTS))
    filtered, margin = pl.pallas_call(
        filter_kernel,
        out_shape=(jax.ShapeDtypeStruct((NODES, COLS), f32), jax.ShapeDtypeStruct((64, COLS), f32)),
        in_specs=[smem] * 2 + [vmem] * 11,
        out_specs=(vmem, vmem),
        scratch_shapes=[
            V((slot_rows, 128), f32),
            V((TERMS, 128), f32),
            V((slot_rows, NODES), f32),
            V((slot_rows, NODES), bf16),
            V((slot_rows, NODES), bf16),
            V((NODES, slot_rows), bf16),
            V((NODES, slot_rows), bf16),
            V((ROWS, slot_rows), bf16),
            V((slot_rows, ROWS), bf16),
            V((CELLS * CELL, NODES), bf16),
            V((NODES, CELLS * CELL), bf16),
            V((2 * FACE, NODES), bf16),
            V((NODES, 2 * FACE), bf16),
            V((TERMS, ROWS), bf16),
            V((ROWS, TERMS), bf16),
            V((TERMS, TERMS), bf16),
            V((TERMS, TERMS), bf16),
            V((NODES, COLS), bf16),
            V((NODES, COLS), bf16),
            V((ROWS, 128), bf16),
            V((ROWS, 128), bf16),
            V((CELLS * CELL, COLS), bf16),
            V((CELLS * CELL, COLS), bf16),
            V((CELLS * CELL, COLS), bf16),
            V((CELLS * CELL, COLS), bf16),
            V((NODES, COLS), f32),
            V((NODES, COLS), f32),
            V((2, PARTS, WIDE, 128), f32),
            V((2, PARTS, WIDE, 128), f32),
            V((2, PARTS, WIDE, 128), f32),
            V((2, PARTS, WIDE, 128), f32),
            V((PARTS, 8, 128), f32),
            V((PARTS, 8, 128), f32),
            V((2 * FACE, COLS), f32),
            V((3, 2 * FACE, COLS), f32),
            pairs,
            pairs,
            pairs,
            pairs,
            D((PARTS,)),
            D((PARTS,)),
            D((2,)),
            D((3, 2)),
            V((COLS, NODES), bf16),
            V((COLS, NODES), bf16),
            V((COLS, COLS), f32),
            V((7, NODES // 2, COLS), f32),
            V((GROUPS, 2, 128, 128), f32),
            V((GROUPS, 2, 128, 128), f32),
            V((GROUPS, 2, 128, 128), f32),
            V((PARTS // 2, 128, 128), f32),
            V((128, 128), f32),
            V((4, 64, 128), f32),
            D((7,)),
            D((7,)),
            D((GROUPS,)),
            D((GROUPS,)),
            D((GROUPS, 2)),
            D((PARTS // 2,)),
            D((4,)),
            D((4,)),
        ],
        compiler_params=pltpu.CompilerParams(
            collective_id=0, has_side_effects=True, vmem_limit_bytes=58 * 2**20
        ),
        name="filter_bands",
    )(
        filter_center,
        filter_half,
        bands_in,
        cell_ham,
        cell_nodes,
        left_face,
        right_face,
        jnp.transpose(proj_values, (1, 0, 2)),
        proj_nodes,
        slot_owner.reshape(1, SLOTS),
        slot_atom.reshape(1, SLOTS),
        jnp.transpose(coupling, (1, 0, 2)),
        node_weight.reshape(1, NODES),
    )
    return filtered, margin.T


def per_device(
    bands_in,
    cell_ham,
    cell_nodes,
    left_face,
    right_face,
    proj_values,
    proj_nodes,
    slot_owner,
    slot_atom,
    coupling,
    node_weight,
    filter_center,
    filter_half,
):
    return run_filter(
        bands_in, cell_ham, cell_nodes, left_face, right_face, proj_values, proj_nodes, slot_owner, slot_atom, coupling,
        node_weight, filter_center, filter_half,
    )


def solution(mesh):
    placed = (
        P("mesh", "band"),
        P("mesh", None, None),
        P("mesh", None),
        P("mesh", None),
        P("mesh", None),
        P("mesh", None, None),
        P("mesh", None),
        P("mesh", None),
        P("mesh"),
        P("mesh", None, None),
        P("mesh"),
        P(),
        P(),
    )
    return jax.shard_map(
        per_device,
        mesh=mesh,
        in_specs=placed,
        out_specs=(P("mesh", "band"), P("band", "mesh")),
        check_vma=False,
    )
```

```python
import jax
import jax.numpy as jnp
from jax import lax
from jax.experimental import pallas as pl
from jax.experimental.pallas import tpu as pltpu
from jax.sharding import PartitionSpec as P

MESH = pl.DeviceIdType.MESH
f32, bf16, i32 = jnp.float32, jnp.bfloat16, jnp.int32

PARTS = 32
NODES = 1024
COLS = 256
SLOTS = 32
PROJ = 18
PADDED = 24
ATOMS = 16
CELLS = 3
CELL = 512
FACE = 128
WIDE = 40
ROWS = PARTS * WIDE
TERMS = ATOMS * PADDED
BLOCK = 256
GROUPS = 8


def mm(a, b):
    return jnp.dot(a, b, preferred_element_type=f32)


def split(x):
    high = x.astype(bf16)
    return high, (x - high.astype(f32)).astype(bf16)


def iota(shape, dim):
    return lax.broadcasted_iota(i32, shape, dim)


def hot(mask):
    return jnp.where(mask, 1.0, 0.0).astype(bf16)


def rows_at(index, size=BLOCK):
    return pl.ds(pl.multiple_of(index * size, size), size)


def loop(count, body):
    def step(i, carry):
        body(i)
        return carry

    lax.fori_loop(0, count, step, 0)


def filter_kernel(
    centre_ref,
    half_ref,
    bands_in,
    cell_ham,
    cell_nodes,
    left_face,
    right_face,
    proj_values,
    proj_nodes,
    slot_owner,
    slot_atom,
    coupling,
    node_weight,
    filtered,
    margin,
    stacked,
    coupled,
    b24,
    b24h,
    b24l,
    b24th,
    b24tl,
    place,
    placet,
    gat,
    sca,
    fgat,
    fsca,
    member,
    memt,
    cbh,
    cbl,
    vh,
    vl,
    xh,
    xl,
    gh,
    gl,
    ph,
    plo,
    cells,
    previous,
    out1,
    in1,
    out2,
    in2,
    labels,
    lab_in,
    face_out,
    face_in,
    s1,
    r1,
    s2,
    r2,
    sl,
    rl,
    sf,
    rf,
    wth,
    wtl,
    product,
    halves,
    kept,
    given,
    core_in,
    strips,
    turned,
    swapped,
    sh,
    rh,
    sc,
    rc,
    ss,
    rs,
    sw,
    rw,
):
    me = lax.axis_index("mesh")
    band = lax.axis_index("band")
    other = me // 4
    quarter = lax.rem(me, 4)
    centre, half = centre_ref[0], half_ref[0]

    def peer(k):
        return lax.rem(me + k, PARTS)

    face_in[...] = jnp.zeros_like(face_in)
    in1[...] = jnp.zeros_like(in1)
    in2[...] = jnp.zeros_like(in2)
    barrier = pltpu.get_barrier_semaphore()

    def greet(k):
        pl.semaphore_signal(barrier, inc=1, device_id=(band, peer(k + 1)), device_id_type=MESH)

    loop(PARTS - 1, greet)

    def greet_group(k):
        group = lax.rem(band + k + 1, GROUPS)
        pl.semaphore_signal(barrier, inc=1, device_id=(group, me), device_id_type=MESH)

    loop(GROUPS - 1, greet_group)

    @pl.when(other != band)
    def _():
        def greet_mirror(j):
            pl.semaphore_signal(barrier, inc=1, device_id=(other, band * 4 + j), device_id_type=MESH)

        loop(4, greet_mirror)

    stacked[...] = jnp.zeros_like(stacked)
    for s in range(SLOTS):
        stacked[s * PADDED : s * PADDED + PROJ, :] = proj_values[:, s, :]
    slot_cols = proj_nodes[...].astype(f32).T
    node = iota((128, NODES), 1).astype(f32)
    upper = lax.rem(iota((4 * PADDED, 128), 0), 2 * PADDED) < PADDED
    for t in range(SLOTS // 2):
        at = slice(t * 2 * PADDED, (t + 1) * 2 * PADDED)
        spread = jnp.concatenate([hot(slot_cols[:, s : s + 1] == node) for s in (2 * t, 2 * t + 1)], axis=0)
        values = stacked[at, :]
        high = values.astype(bf16).astype(f32)
        both = jnp.concatenate([high, values - high], axis=0)
        both = jnp.concatenate([jnp.where(upper, both, 0.0), jnp.where(upper, 0.0, both)], axis=1)
        result = mm(both.astype(bf16), spread)
        b24[at, :] = result[: 2 * PADDED] + result[2 * PADDED :]
    high, low = split(b24[...])
    b24h[...] = high
    b24l[...] = low

    owner_row = slot_owner[...].astype(f32)
    atom_row = slot_atom[...].astype(f32)
    down, across = iota((SLOTS, SLOTS), 0), iota((SLOTS, SLOTS), 1)
    owner_col = jnp.sum(jnp.where(down == across, owner_row, 0.0), axis=1, keepdims=True)
    earlier = jnp.where((owner_col == owner_row) & (across < down), 1.0, 0.0)
    bucket_col = 2.0 * owner_col + jnp.sum(earlier, axis=1, keepdims=True)
    bucket_row = jnp.sum(jnp.where(down == across, bucket_col, 0.0), axis=0, keepdims=True)
    shape = (SLOTS, SLOTS * PADDED)
    spot = jnp.sum(jnp.where(iota(shape, 0) == iota(shape, 1) // PADDED, bucket_col, 0.0), axis=0, keepdims=True)
    lane = lax.rem(iota((1, SLOTS * PADDED), 1), PADDED)
    spot = jnp.where(lane < PROJ, spot.astype(i32) * PADDED + lane, -2)
    shape = (SLOTS * PADDED, SLOTS)
    spot_col = jnp.sum(jnp.where(iota(shape, 1) == iota(shape, 0) // PADDED, bucket_row, 0.0), axis=1, keepdims=True)
    lane = lax.rem(iota((SLOTS * PADDED, 1), 0), PADDED)
    spot_col = jnp.where(lane < PROJ, spot_col.astype(i32) * PADDED + lane, -2)

    def row_key(row):
        number = lax.rem(row, WIDE)
        key = (2 * (row // WIDE) + number // PROJ) * PADDED + lax.rem(number, PROJ)
        return jnp.where(number < 2 * PROJ, key, -1)

    for i in range(ROWS // BLOCK):
        at = slice(i * BLOCK, (i + 1) * BLOCK)
        place[at, :] = hot(row_key(iota((BLOCK, 1), 0) + i * BLOCK) == spot)

    previous[...] = bands_in[...]
    filtered[...] = bands_in[...]
    high, low = split(bands_in[...])
    vh[...] = high
    vl[...] = low

    def sides(h):
        return slice(h * 128, (h + 1) * 128)

    def copy_to(source, target, send, receive, h, o):
        return pltpu.make_async_remote_copy(
            source.at[h, o, pl.ds(0, 2 * PROJ)],
            target.at[h, me, pl.ds(0, 2 * PROJ)],
            send.at[h, o],
            receive.at[h, me],
            device_id=(band, o),
            device_id_type=MESH,
        )

    def arrival(source, target, send, receive, h, q):
        return pltpu.make_async_remote_copy(
            source.at[h, q, pl.ds(0, 2 * PROJ)],
            target.at[h, q, pl.ds(0, 2 * PROJ)],
            send.at[h, q],
            receive.at[h, q],
            device_id=(band, q),
            device_id_type=MESH,
        )

    def exchange(h, rows_of, out, target, send, receive):
        def group(t):
            g = lax.rem(me // 16 + 1 + t, 2)
            out[h, pl.ds(g * 16, 16)] = rows_of(rows_at(g, ROWS // 2)).reshape(16, WIDE, 128)

            def one(i):
                o = g * 16 + lax.rem(me + i, 16)

                @pl.when(o != me)
                def _():
                    copy_to(out, target, send, receive, h, o).start()

            loop(16, one)

        loop(2, group)
        target[h, me] = out[h, me]

    def collect(h, out, target, send, receive):
        def one(k):
            arrival(out, target, send, receive, h, peer(k + 1)).wait_recv()

        loop(PARTS - 1, one)
        high, low = split(target[h].reshape(ROWS, 128))
        xh[...] = high
        xl[...] = low

    def sent(h, out, target, send, receive):
        def one(k):
            arrival(out, target, send, receive, h, peer(k + 1)).wait_send()

        loop(PARTS - 1, one)

    def send_coefficients(h):
        columns = sides(h)
        fh, fl = vh[:, columns], vl[:, columns]
        high, low = split(mm(b24h[...], fh) + (mm(b24h[...], fl) + mm(b24l[...], fh)))
        exchange(h, lambda at: mm(place[at, :], high) + mm(place[at, :], low), out1, in1, s1, r1)

    pl.semaphore_wait(barrier, jnp.where(other != band, 4, 0) + PARTS - 1 + GROUPS - 1)
    for h in range(2):
        send_coefficients(h)

    target = iota((PARTS, SLOTS), 0).astype(f32) * 2.0
    first = jnp.sum(jnp.where(bucket_row == target, atom_row + 1.0, 0.0), axis=1, keepdims=True) - 1.0
    second = jnp.sum(jnp.where(bucket_row == target + 1.0, atom_row + 1.0, 0.0), axis=1, keepdims=True) - 1.0
    lane = iota((PARTS, 128), 1)
    named = jnp.where(lane < PROJ, first, jnp.where(lane < 2 * PROJ, second, -1.0))
    for o in range(PARTS):
        labels[o] = jnp.broadcast_to(named[o : o + 1, :], (8, 128))

    def label_to(o):
        return pltpu.make_async_remote_copy(
            labels.at[o], lab_in.at[me], sl.at[o], rl.at[me], device_id=(band, o), device_id_type=MESH
        )

    def label_from(q):
        return pltpu.make_async_remote_copy(
            labels.at[q], lab_in.at[q], sl.at[q], rl.at[q], device_id=(band, q), device_id_type=MESH
        )

    def tell(k):
        label_to(peer(k + 1)).start()

    loop(PARTS - 1, tell)
    lab_in[me] = labels[me]

    for i in range(NODES // BLOCK):
        at = slice(i * BLOCK, (i + 1) * BLOCK)
        row = iota((BLOCK, CELL), 0) + i * BLOCK
        for c in range(CELLS):
            mask = jnp.where(row == cell_nodes[c : c + 1, :], 1.0, 0.0)
            sca[at, c * CELL : (c + 1) * CELL] = mask.astype(bf16)
            gat[c * CELL : (c + 1) * CELL, at] = mask.T.astype(bf16)
        for side, face in enumerate((left_face, right_face)):
            mask = jnp.where(row[:, :FACE] == face[...], 1.0, 0.0)
            fsca[at, side * FACE : (side + 1) * FACE] = mask.astype(bf16)
            fgat[side * FACE : (side + 1) * FACE, at] = mask.T.astype(bf16)
    for i in range(SLOTS * PADDED // BLOCK):
        at = slice(i * BLOCK, (i + 1) * BLOCK)
        high, low = split(b24[at, :].T)
        b24th[:, at] = high
        b24tl[:, at] = low
        placet[at, :] = hot(spot_col[at, :] == row_key(iota((1, ROWS), 1)))
    coupled[...] = jnp.zeros_like(coupled)
    for a in range(ATOMS):
        coupled[a * PADDED : a * PADDED + PROJ, 0:PROJ] = coupling[:, a, :]
    repeat = hot(iota((128, TERMS), 0) == lax.rem(iota((128, TERMS), 1), PADDED))
    same = iota((TERMS, TERMS), 0) // PADDED == iota((TERMS, TERMS), 1) // PADDED
    high, low = split(coupled[...])
    cbh[...] = jnp.where(same, mm(high, repeat), 0.0).astype(bf16)
    cbl[...] = jnp.where(same, mm(low, repeat), 0.0).astype(bf16)

    def told(k):
        label_from(peer(k + 1)).wait()

    loop(PARTS - 1, told)
    number = lax.rem(iota((128, ROWS), 1), WIDE)
    named = mm(lab_in[...].reshape(PARTS * 8, 128).astype(bf16), hot(iota((128, ROWS), 0) == number))
    source = iota((PARTS * 8, ROWS), 1) // WIDE
    atom = jnp.sum(jnp.where(iota((PARTS * 8, ROWS), 0) == source * 8, named, 0.0), axis=0, keepdims=True)
    number = lax.rem(iota((1, ROWS), 1), WIDE)
    key = jnp.where(atom < 0.0, -1, atom.astype(i32) * PADDED + lax.rem(number, PROJ))
    for i in range(ROWS // BLOCK):
        at = slice(i * BLOCK, (i + 1) * BLOCK)
        mask = jnp.where(iota((TERMS, BLOCK), 0) == key[:, at], 1.0, 0.0)
        member[:, at] = mask.astype(bf16)
        memt[at, :] = mask.T.astype(bf16)

    def face_copy(step, low, other):
        source = face_out.at[pl.ds(0 if low else FACE, FACE)]
        target = face_in.at[step, pl.ds(FACE if low else 0, FACE)]
        side = 0 if low else 1
        return pltpu.make_async_remote_copy(
            source, target, sf.at[side], rf.at[step, 1 - side], device_id=(band, other), device_id_type=MESH
        )

    def face_wait(step, low, other):
        source = face_out.at[pl.ds(0 if low else FACE, FACE)]
        target = face_in.at[step, pl.ds(0 if low else FACE, FACE)]
        side = 0 if low else 1
        return pltpu.make_async_remote_copy(
            source, target, sf.at[side], rf.at[step, side], device_id=(band, other), device_id_type=MESH
        )

    def degree(step):
        gain = jnp.where(step == 0, 1.0, 2.0) / half
        keep = jnp.where(step == 0, 0.0, 1.0)

        def pick(c):
            at = rows_at(c, CELL)
            gh[at, :] = mm(gat[at, :], vh[...]).astype(bf16)
            gl[at, :] = mm(gat[at, :], vl[...]).astype(bf16)
            high, low = split(cell_ham[c])
            high, low = split(mm(high, gh[at, :]) + (mm(high, gl[at, :]) + mm(low, gh[at, :])))
            ph[at, :] = high
            plo[at, :] = low

        loop(CELLS, pick)

        def add(i):
            at = rows_at(i, 512)
            cells[at, :] = mm(sca[at, :], ph[...]) + mm(sca[at, :], plo[...])

        loop(NODES // 512, add)
        high, low = split(cells[...])
        gh[0:NODES, :] = high
        gl[0:NODES, :] = low
        face_out[...] = mm(fgat[...], gh[0:NODES, :]) + mm(fgat[...], gl[0:NODES, :])

        @pl.when(me > 0)
        def _():
            face_copy(step, True, me - 1).start()

        @pl.when(me < PARTS - 1)
        def _():
            face_copy(step, False, me + 1).start()

        for h in range(2):
            collect(h, out1, in1, s1, r1)
            high, low = split(mm(member[...], xh[...]) + mm(member[...], xl[...]))
            applied = mm(cbh[...], high) + (mm(cbh[...], low) + mm(cbl[...], high))
            high, low = split(applied)

            @pl.when(step > 0)
            def _():
                sent(h, out2, in2, s2, r2)

            exchange(h, lambda at: mm(memt[at, :], high) + mm(memt[at, :], low), out2, in2, s2, r2)

        @pl.when(me > 0)
        def _():
            face_wait(step, True, me - 1).wait()

        @pl.when(me < PARTS - 1)
        def _():
            face_wait(step, False, me + 1).wait()

        high, low = split(face_in[step])
        gh[0 : 2 * FACE, :] = high
        gl[0 : 2 * FACE, :] = low

        def assemble(i):
            at = rows_at(i, 512)
            summed = cells[at, :] + mm(fsca[at, :], gh[0:256, :]) + mm(fsca[at, :], gl[0:256, :])
            field = filtered[at, :]
            cells[at, :] = (summed - centre * field) * gain - keep * previous[at, :]
            previous[at, :] = field

        loop(NODES // 512, assemble)
        for h in range(2):
            columns = sides(h)
            collect(h, out2, in2, s2, r2)
            bh, bl = split(mm(placet[...], xh[...]) + mm(placet[...], xl[...]))

            def finish(i):
                at = rows_at(i, 512)
                back = mm(b24th[at, :], bh) + (mm(b24th[at, :], bl) + mm(b24tl[at, :], bh))
                field = cells[at, columns] + gain * back
                filtered[at, columns] = field
                high, low = split(field)
                vh[at, columns] = high
                vl[at, columns] = low

            loop(NODES // 512, finish)
            sent(h, out1, in1, s1, r1)

            @pl.when(step < 2)
            def _():
                send_coefficients(h)

            @pl.when(step == 2)
            def _():
                def begin(t):
                    i = lax.rem(t + me // 2, GROUPS)

                    @pl.when(i > 0)
                    def _():
                        half_of(i, h, me, band, filtered, halves, sh, rh).start()

                loop(GROUPS, begin)
                for i in range(NODES // BLOCK):
                    at = slice(i * BLOCK, (i + 1) * BLOCK)
                    high, low = split(filtered[at, columns].T * node_weight[:, at])
                    wth[columns, at] = high
                    wtl[columns, at] = low

    loop(3, degree)
    for h in range(2):
        sent(h, out2, in2, s2, r2)
    margin_of(
        me, band, other, quarter, node_weight, filtered, margin, vh, vl, wth, wtl, product, halves, kept, given, core_in, strips,
        turned, swapped, sh, rh, sc, rc, ss, rs, sw, rw,
    )


def choose(i, values):
    result = values[0]
    for k in range(1, GROUPS):
        result = jnp.where(i == k, values[k], result)
    return result


def apart(i):
    return choose(i, (0, 0, 1, 3, 1, 3, 2, 2)), choose(i, (0, 1, 0, 0, 1, 1, 0, 1))


def group_at(band, dy, dx):
    return lax.rem(band // 2 + dy, 4) * 2 + lax.rem(band + dx, 2)


def half_of(i, h, me, band, filtered, halves, sh, rh):
    x, far = lax.rem(band, 2), band // 4
    mine = choose(i, (0, x, 0, 1, 0, 1, far, far))
    columns = pl.ds(h * 128, 128)
    return pltpu.make_async_remote_copy(
        filtered.at[rows_at(mine, NODES // 2), columns],
        halves.at[i - 1, :, columns],
        sh.at[i - 1, h],
        rh.at[i - 1, h],
        device_id=(group_at(band, *apart(i)), me),
        device_id_type=MESH,
    )


def margin_of(
    me, band, other, quarter, node_weight, filtered, margin, vh, vl, wth, wtl, product, halves, kept, given, core_in, strips,
    turned, swapped, sh, rh, sc, rc, ss, rs, sw, rw,
):
    x, far = lax.rem(band, 2), band // 4
    core, chip = lax.rem(me, 2), me // 2
    sibling = me + 1 - 2 * core

    def block_at(t):
        return lax.rem(t + chip, GROUPS)

    def owner(i):
        dy, dx = apart(i)
        return group_at(band, 4 - dy, dx)

    def half_copy(i, h):
        return half_of(i, h, me, band, filtered, halves, sh, rh)

    def core_copy(i):
        return pltpu.make_async_remote_copy(
            given.at[i], core_in.at[i], sc.at[i], rc.at[i], device_id=(band, sibling), device_id_type=MESH
        )

    def strip_copy(i, j, target):
        return pltpu.make_async_remote_copy(
            kept.at[i, j], strips.at[chip], ss.at[i, j], rs.at[chip], device_id=(band, target), device_id_type=MESH
        )

    lower = iota((128, 128), 1) < 64

    def send_strips(i):
        core_copy(i).wait_recv()
        for j in range(2):
            kept[i, j] = kept[i, j] + core_in[i, j]
            target = owner(i) * 4 + 2 * j + core

            @pl.when(target == me)
            def _():
                strips[chip] = kept[i, j]

            @pl.when(target != me)
            def _():
                strip_copy(i, j, target).start()

    def multiply(t):
        i = block_at(t)

        @pl.when(i == 0)
        def _():
            product[...] = mm(wth[...], vh[...]) + (mm(wth[...], vl[...]) + mm(wtl[...], vh[...]))

        @pl.when(i > 0)
        def _():
            for h in range(2):
                half_copy(i, h).wait_recv()
            at = rows_at(choose(i, (0, 1 - x, 0, 1, 0, 1, 1 - far, 1 - far)), NODES // 2)
            high, low = split(halves[i - 1])
            product[...] = mm(wth[:, at], high) + (mm(wth[:, at], low) + mm(wtl[:, at], high))

        for j in range(2):
            top, bottom = product[:128, j * 128 : (j + 1) * 128], product[128:, j * 128 : (j + 1) * 128]
            even = jnp.where(lower, top, pltpu.roll(bottom, 64, 1))
            odd = jnp.where(lower, pltpu.roll(top, 64, 1), bottom)
            kept[i, j] = jnp.where(core == 0, even, odd)
            given[i, j] = jnp.where(core == 0, odd, even)
        core_copy(i).start()

        @pl.when(t > 0)
        def _():
            send_strips(block_at(t + GROUPS - 1))

    loop(GROUPS, multiply)
    send_strips(block_at(GROUPS - 1))

    def arrived(k):
        source = lax.rem(chip + k + 1, PARTS // 2)
        pltpu.make_async_remote_copy(
            kept.at[0, 0], strips.at[source], ss.at[0, 0], rs.at[source], device_id=(band, source * 2 + core), device_id_type=MESH
        ).wait_recv()

    loop(PARTS // 2 - 1, arrived)
    total = jnp.sum(strips[...], axis=0)
    flipped = total.T
    margin[:, :128] = flipped[:64]
    margin[:, 128:] = flipped[64:]

    def swap_copy(j):
        return pltpu.make_async_remote_copy(
            turned.at[pl.ds(64 * (j % 2), 64)],
            swapped.at[quarter],
            sw.at[j],
            rw.at[quarter],
            device_id=(other, band * 4 + j),
            device_id_type=MESH,
        )

    @pl.when(other != band)
    def _():
        turned[...] = total
        for j in range(4):
            swap_copy(j).start()
        for j in range(4):
            pltpu.make_async_remote_copy(
                turned.at[pl.ds(0, 64)], swapped.at[j], sw.at[j], rw.at[j], device_id=(other, band * 4 + j), device_id_type=MESH
            ).wait_recv()
        lowest = iota((64, 128), 1) < 64
        for j in range(2):
            even, odd = swapped[2 * j], swapped[2 * j + 1]
            left = jnp.where(lowest, even, pltpu.roll(odd, 64, 1))
            right = jnp.where(lowest, pltpu.roll(even, 64, 1), odd)
            margin[:, j * 128 : (j + 1) * 128] += jnp.where(quarter < 2, left, right)
        for j in range(4):
            swap_copy(j).wait_send()

    def finished(i):
        @pl.when(i > 0)
        def _():
            for h in range(2):
                half_copy(i, h).wait_send()

        core_copy(i).wait_send()
        for j in range(2):
            target = owner(i) * 4 + 2 * j + core

            @pl.when(target != me)
            def _():
                strip_copy(i, j, target).wait_send()

    loop(GROUPS, finished)


def run_filter(
    bands_in, cell_ham, cell_nodes, left_face, right_face, proj_values, proj_nodes, slot_owner, slot_atom, coupling, node_weight,
    filter_center, filter_half,
):
    vmem = pl.BlockSpec(memory_space=pltpu.VMEM)
    smem = pl.BlockSpec(memory_space=pltpu.SMEM)
    D = pltpu.SemaphoreType.DMA
    V = pltpu.VMEM
    slot_rows = SLOTS * PADDED
    pairs = D((2, PARTS))
    filtered, margin = pl.pallas_call(
        filter_kernel,
        out_shape=(jax.ShapeDtypeStruct((NODES, COLS), f32), jax.ShapeDtypeStruct((64, COLS), f32)),
        in_specs=[smem] * 2 + [vmem] * 11,
        out_specs=(vmem, vmem),
        scratch_shapes=[
            V((slot_rows, 128), f32),
            V((TERMS, 128), f32),
            V((slot_rows, NODES), f32),
            V((slot_rows, NODES), bf16),
            V((slot_rows, NODES), bf16),
            V((NODES, slot_rows), bf16),
            V((NODES, slot_rows), bf16),
            V((ROWS, slot_rows), bf16),
            V((slot_rows, ROWS), bf16),
            V((CELLS * CELL, NODES), bf16),
            V((NODES, CELLS * CELL), bf16),
            V((2 * FACE, NODES), bf16),
            V((NODES, 2 * FACE), bf16),
            V((TERMS, ROWS), bf16),
            V((ROWS, TERMS), bf16),
            V((TERMS, TERMS), bf16),
            V((TERMS, TERMS), bf16),
            V((NODES, COLS), bf16),
            V((NODES, COLS), bf16),
            V((ROWS, 128), bf16),
            V((ROWS, 128), bf16),
            V((CELLS * CELL, COLS), bf16),
            V((CELLS * CELL, COLS), bf16),
            V((CELLS * CELL, COLS), bf16),
            V((CELLS * CELL, COLS), bf16),
            V((NODES, COLS), f32),
            V((NODES, COLS), f32),
            V((2, PARTS, WIDE, 128), f32),
            V((2, PARTS, WIDE, 128), f32),
            V((2, PARTS, WIDE, 128), f32),
            V((2, PARTS, WIDE, 128), f32),
            V((PARTS, 8, 128), f32),
            V((PARTS, 8, 128), f32),
            V((2 * FACE, COLS), f32),
            V((3, 2 * FACE, COLS), f32),
            pairs,
            pairs,
            pairs,
            pairs,
            D((PARTS,)),
            D((PARTS,)),
            D((2,)),
            D((3, 2)),
            V((COLS, NODES), bf16),
            V((COLS, NODES), bf16),
            V((COLS, COLS), f32),
            V((7, NODES // 2, COLS), f32),
            V((GROUPS, 2, 128, 128), f32),
            V((GROUPS, 2, 128, 128), f32),
            V((GROUPS, 2, 128, 128), f32),
            V((PARTS // 2, 128, 128), f32),
            V((128, 128), f32),
            V((4, 64, 128), f32),
            D((7, 2)),
            D((7, 2)),
            D((GROUPS,)),
            D((GROUPS,)),
            D((GROUPS, 2)),
            D((PARTS // 2,)),
            D((4,)),
            D((4,)),
        ],
        compiler_params=pltpu.CompilerParams(
            collective_id=0, has_side_effects=True, vmem_limit_bytes=58 * 2**20
        ),
        name="filter_bands",
    )(
        filter_center,
        filter_half,
        bands_in,
        cell_ham,
        cell_nodes,
        left_face,
        right_face,
        jnp.transpose(proj_values, (1, 0, 2)),
        proj_nodes,
        slot_owner.reshape(1, SLOTS),
        slot_atom.reshape(1, SLOTS),
        jnp.transpose(coupling, (1, 0, 2)),
        node_weight.reshape(1, NODES),
    )
    return filtered, margin.T


def per_device(
    bands_in,
    cell_ham,
    cell_nodes,
    left_face,
    right_face,
    proj_values,
    proj_nodes,
    slot_owner,
    slot_atom,
    coupling,
    node_weight,
    filter_center,
    filter_half,
):
    return run_filter(
        bands_in, cell_ham, cell_nodes, left_face, right_face, proj_values, proj_nodes, slot_owner, slot_atom, coupling,
        node_weight, filter_center, filter_half,
    )


def solution(mesh):
    placed = (
        P("mesh", "band"),
        P("mesh", None, None),
        P("mesh", None),
        P("mesh", None),
        P("mesh", None),
        P("mesh", None, None),
        P("mesh", None),
        P("mesh", None),
        P("mesh"),
        P("mesh", None, None),
        P("mesh"),
        P(),
        P(),
    )
    return jax.shard_map(
        per_device,
        mesh=mesh,
        in_specs=placed,
        out_specs=(P("mesh", "band"), P("band", "mesh")),
        check_vma=False,
    )
```

```python
import jax
import jax.numpy as jnp
from jax import lax
from jax.experimental import pallas as pl
from jax.experimental.pallas import tpu as pltpu
from jax.sharding import PartitionSpec as P

MESH = pl.DeviceIdType.MESH
f32, bf16, i32 = jnp.float32, jnp.bfloat16, jnp.int32

PARTS = 32
NODES = 1024
COLS = 256
SLOTS = 32
PROJ = 18
PADDED = 24
ATOMS = 16
CELLS = 3
CELL = 512
FACE = 128
WIDE = 40
ROWS = PARTS * WIDE
TERMS = ATOMS * PADDED
BLOCK = 256
GROUPS = 8


def mm(a, b):
    return jnp.dot(a, b, preferred_element_type=f32)


def split(x):
    high = x.astype(bf16)
    return high, (x - high.astype(f32)).astype(bf16)


def iota(shape, dim):
    return lax.broadcasted_iota(i32, shape, dim)


def hot(mask):
    return jnp.where(mask, 1.0, 0.0).astype(bf16)


def rows_at(index, size=BLOCK):
    return pl.ds(pl.multiple_of(index * size, size), size)


def loop(count, body):
    def step(i, carry):
        body(i)
        return carry

    lax.fori_loop(0, count, step, 0)


def filter_kernel(
    centre_ref,
    half_ref,
    bands_in,
    cell_ham,
    cell_nodes,
    left_face,
    right_face,
    proj_values,
    proj_nodes,
    slot_owner,
    slot_atom,
    coupling,
    node_weight,
    filtered,
    margin,
    stacked,
    coupled,
    b24,
    b24h,
    b24l,
    b24th,
    b24tl,
    place,
    placet,
    gat,
    sca,
    fgat,
    fsca,
    member,
    memt,
    cbh,
    cbl,
    vh,
    vl,
    xh,
    xl,
    gh,
    gl,
    ph,
    plo,
    cells,
    previous,
    out1,
    in1,
    out2,
    in2,
    labels,
    lab_in,
    face_out,
    face_in,
    s1,
    r1,
    s2,
    r2,
    sl,
    rl,
    sf,
    rf,
    wth,
    wtl,
    product,
    halves,
    kept,
    given,
    core_in,
    strips,
    turned,
    swapped,
    sh,
    rh,
    sc,
    rc,
    ss,
    rs,
    sw,
    rw,
):
    me = lax.axis_index("mesh")
    band = lax.axis_index("band")
    other = me // 4
    quarter = lax.rem(me, 4)
    centre, half = centre_ref[0], half_ref[0]

    def peer(k):
        return lax.rem(me + k, PARTS)

    face_in[...] = jnp.zeros_like(face_in)
    in1[...] = jnp.zeros_like(in1)
    in2[...] = jnp.zeros_like(in2)
    barrier = pltpu.get_barrier_semaphore()

    def greet(k):
        pl.semaphore_signal(barrier, inc=1, device_id=(band, peer(k + 1)), device_id_type=MESH)

    loop(PARTS - 1, greet)

    def greet_group(k):
        group = lax.rem(band + k + 1, GROUPS)
        pl.semaphore_signal(barrier, inc=1, device_id=(group, me), device_id_type=MESH)

    loop(GROUPS - 1, greet_group)

    @pl.when(other != band)
    def _():
        def greet_mirror(j):
            pl.semaphore_signal(barrier, inc=1, device_id=(other, band * 4 + j), device_id_type=MESH)

        loop(4, greet_mirror)

    stacked[...] = jnp.zeros_like(stacked)
    for s in range(SLOTS):
        stacked[s * PADDED : s * PADDED + PROJ, :] = proj_values[:, s, :]
    slot_cols = proj_nodes[...].astype(f32).T
    node = iota((128, NODES), 1).astype(f32)
    upper = lax.rem(iota((4 * PADDED, 128), 0), 2 * PADDED) < PADDED
    for t in range(SLOTS // 2):
        at = slice(t * 2 * PADDED, (t + 1) * 2 * PADDED)
        spread = jnp.concatenate([hot(slot_cols[:, s : s + 1] == node) for s in (2 * t, 2 * t + 1)], axis=0)
        values = stacked[at, :]
        high = values.astype(bf16).astype(f32)
        both = jnp.concatenate([high, values - high], axis=0)
        both = jnp.concatenate([jnp.where(upper, both, 0.0), jnp.where(upper, 0.0, both)], axis=1)
        result = mm(both.astype(bf16), spread)
        b24[at, :] = result[: 2 * PADDED] + result[2 * PADDED :]
    high, low = split(b24[...])
    b24h[...] = high
    b24l[...] = low

    owner_row = slot_owner[...].astype(f32)
    atom_row = slot_atom[...].astype(f32)
    down, across = iota((SLOTS, SLOTS), 0), iota((SLOTS, SLOTS), 1)
    owner_col = jnp.sum(jnp.where(down == across, owner_row, 0.0), axis=1, keepdims=True)
    earlier = jnp.where((owner_col == owner_row) & (across < down), 1.0, 0.0)
    bucket_col = 2.0 * owner_col + jnp.sum(earlier, axis=1, keepdims=True)
    bucket_row = jnp.sum(jnp.where(down == across, bucket_col, 0.0), axis=0, keepdims=True)
    shape = (SLOTS, SLOTS * PADDED)
    spot = jnp.sum(jnp.where(iota(shape, 0) == iota(shape, 1) // PADDED, bucket_col, 0.0), axis=0, keepdims=True)
    lane = lax.rem(iota((1, SLOTS * PADDED), 1), PADDED)
    spot = jnp.where(lane < PROJ, spot.astype(i32) * PADDED + lane, -2)
    shape = (SLOTS * PADDED, SLOTS)
    spot_col = jnp.sum(jnp.where(iota(shape, 1) == iota(shape, 0) // PADDED, bucket_row, 0.0), axis=1, keepdims=True)
    lane = lax.rem(iota((SLOTS * PADDED, 1), 0), PADDED)
    spot_col = jnp.where(lane < PROJ, spot_col.astype(i32) * PADDED + lane, -2)

    def row_key(row):
        number = lax.rem(row, WIDE)
        key = (2 * (row // WIDE) + number // PROJ) * PADDED + lax.rem(number, PROJ)
        return jnp.where(number < 2 * PROJ, key, -1)

    for i in range(ROWS // BLOCK):
        at = slice(i * BLOCK, (i + 1) * BLOCK)
        place[at, :] = hot(row_key(iota((BLOCK, 1), 0) + i * BLOCK) == spot)

    previous[...] = bands_in[...]
    filtered[...] = bands_in[...]
    high, low = split(bands_in[...])
    vh[...] = high
    vl[...] = low

    def sides(h):
        return slice(h * 128, (h + 1) * 128)

    def copy_to(source, target, send, receive, h, o):
        return pltpu.make_async_remote_copy(
            source.at[h, o, pl.ds(0, 2 * PROJ)],
            target.at[h, me, pl.ds(0, 2 * PROJ)],
            send.at[h, o],
            receive.at[h, me],
            device_id=(band, o),
            device_id_type=MESH,
        )

    def arrival(source, target, send, receive, h, q):
        return pltpu.make_async_remote_copy(
            source.at[h, q, pl.ds(0, 2 * PROJ)],
            target.at[h, q, pl.ds(0, 2 * PROJ)],
            send.at[h, q],
            receive.at[h, q],
            device_id=(band, q),
            device_id_type=MESH,
        )

    def exchange(h, rows_of, out, target, send, receive):
        def group(t):
            g = lax.rem(me // 16 + 1 + t, 2)
            out[h, pl.ds(g * 16, 16)] = rows_of(rows_at(g, ROWS // 2)).reshape(16, WIDE, 128)

            def one(i):
                o = g * 16 + lax.rem(me + i, 16)

                @pl.when(o != me)
                def _():
                    copy_to(out, target, send, receive, h, o).start()

            loop(16, one)

        loop(2, group)
        target[h, me] = out[h, me]

    def collect(h, out, target, send, receive):
        def one(k):
            arrival(out, target, send, receive, h, peer(k + 1)).wait_recv()

        loop(PARTS - 1, one)
        high, low = split(target[h].reshape(ROWS, 128))
        xh[...] = high
        xl[...] = low

    def sent(h, out, target, send, receive):
        def one(k):
            arrival(out, target, send, receive, h, peer(k + 1)).wait_send()

        loop(PARTS - 1, one)

    def send_coefficients(h):
        columns = sides(h)
        fh, fl = vh[:, columns], vl[:, columns]
        high, low = split(mm(b24h[...], fh) + (mm(b24h[...], fl) + mm(b24l[...], fh)))
        exchange(h, lambda at: mm(place[at, :], high) + mm(place[at, :], low), out1, in1, s1, r1)

    pl.semaphore_wait(barrier, jnp.where(other != band, 4, 0) + PARTS - 1 + GROUPS - 1)
    for h in range(2):
        send_coefficients(h)

    target = iota((PARTS, SLOTS), 0).astype(f32) * 2.0
    first = jnp.sum(jnp.where(bucket_row == target, atom_row + 1.0, 0.0), axis=1, keepdims=True) - 1.0
    second = jnp.sum(jnp.where(bucket_row == target + 1.0, atom_row + 1.0, 0.0), axis=1, keepdims=True) - 1.0
    lane = iota((PARTS, 128), 1)
    named = jnp.where(lane < PROJ, first, jnp.where(lane < 2 * PROJ, second, -1.0))
    for o in range(PARTS):
        labels[o] = jnp.broadcast_to(named[o : o + 1, :], (8, 128))

    def label_to(o):
        return pltpu.make_async_remote_copy(
            labels.at[o], lab_in.at[me], sl.at[o], rl.at[me], device_id=(band, o), device_id_type=MESH
        )

    def label_from(q):
        return pltpu.make_async_remote_copy(
            labels.at[q], lab_in.at[q], sl.at[q], rl.at[q], device_id=(band, q), device_id_type=MESH
        )

    def tell(k):
        label_to(peer(k + 1)).start()

    loop(PARTS - 1, tell)
    lab_in[me] = labels[me]

    for i in range(NODES // BLOCK):
        at = slice(i * BLOCK, (i + 1) * BLOCK)
        row = iota((BLOCK, CELL), 0) + i * BLOCK
        for c in range(CELLS):
            mask = jnp.where(row == cell_nodes[c : c + 1, :], 1.0, 0.0)
            sca[at, c * CELL : (c + 1) * CELL] = mask.astype(bf16)
            gat[c * CELL : (c + 1) * CELL, at] = mask.T.astype(bf16)
        for side, face in enumerate((left_face, right_face)):
            mask = jnp.where(row[:, :FACE] == face[...], 1.0, 0.0)
            fsca[at, side * FACE : (side + 1) * FACE] = mask.astype(bf16)
            fgat[side * FACE : (side + 1) * FACE, at] = mask.T.astype(bf16)
    for i in range(SLOTS * PADDED // BLOCK):
        at = slice(i * BLOCK, (i + 1) * BLOCK)
        high, low = split(b24[at, :].T)
        b24th[:, at] = high
        b24tl[:, at] = low
        placet[at, :] = hot(spot_col[at, :] == row_key(iota((1, ROWS), 1)))
    coupled[...] = jnp.zeros_like(coupled)
    for a in range(ATOMS):
        coupled[a * PADDED : a * PADDED + PROJ, 0:PROJ] = coupling[:, a, :]
    repeat = hot(iota((128, TERMS), 0) == lax.rem(iota((128, TERMS), 1), PADDED))
    same = iota((TERMS, TERMS), 0) // PADDED == iota((TERMS, TERMS), 1) // PADDED
    high, low = split(coupled[...])
    cbh[...] = jnp.where(same, mm(high, repeat), 0.0).astype(bf16)
    cbl[...] = jnp.where(same, mm(low, repeat), 0.0).astype(bf16)

    def told(k):
        label_from(peer(k + 1)).wait()

    loop(PARTS - 1, told)
    number = lax.rem(iota((128, ROWS), 1), WIDE)
    named = mm(lab_in[...].reshape(PARTS * 8, 128).astype(bf16), hot(iota((128, ROWS), 0) == number))
    source = iota((PARTS * 8, ROWS), 1) // WIDE
    atom = jnp.sum(jnp.where(iota((PARTS * 8, ROWS), 0) == source * 8, named, 0.0), axis=0, keepdims=True)
    number = lax.rem(iota((1, ROWS), 1), WIDE)
    key = jnp.where(atom < 0.0, -1, atom.astype(i32) * PADDED + lax.rem(number, PROJ))
    for i in range(ROWS // BLOCK):
        at = slice(i * BLOCK, (i + 1) * BLOCK)
        mask = jnp.where(iota((TERMS, BLOCK), 0) == key[:, at], 1.0, 0.0)
        member[:, at] = mask.astype(bf16)
        memt[at, :] = mask.T.astype(bf16)

    def face_copy(step, low, other):
        source = face_out.at[pl.ds(0 if low else FACE, FACE)]
        target = face_in.at[step, pl.ds(FACE if low else 0, FACE)]
        side = 0 if low else 1
        return pltpu.make_async_remote_copy(
            source, target, sf.at[side], rf.at[step, 1 - side], device_id=(band, other), device_id_type=MESH
        )

    def face_wait(step, low, other):
        source = face_out.at[pl.ds(0 if low else FACE, FACE)]
        target = face_in.at[step, pl.ds(0 if low else FACE, FACE)]
        side = 0 if low else 1
        return pltpu.make_async_remote_copy(
            source, target, sf.at[side], rf.at[step, side], device_id=(band, other), device_id_type=MESH
        )

    def degree(step):
        gain = jnp.where(step == 0, 1.0, 2.0) / half
        keep = jnp.where(step == 0, 0.0, 1.0)

        def pick(c):
            at = rows_at(c, CELL)
            gh[at, :] = mm(gat[at, :], vh[...]).astype(bf16)
            gl[at, :] = mm(gat[at, :], vl[...]).astype(bf16)
            high, low = split(cell_ham[c])
            high, low = split(mm(high, gh[at, :]) + (mm(high, gl[at, :]) + mm(low, gh[at, :])))
            ph[at, :] = high
            plo[at, :] = low

        loop(CELLS, pick)

        def add(i):
            at = rows_at(i, 512)
            cells[at, :] = mm(sca[at, :], ph[...]) + mm(sca[at, :], plo[...])

        loop(NODES // 512, add)
        high, low = split(cells[...])
        gh[0:NODES, :] = high
        gl[0:NODES, :] = low
        face_out[...] = mm(fgat[...], gh[0:NODES, :]) + mm(fgat[...], gl[0:NODES, :])

        @pl.when(me > 0)
        def _():
            face_copy(step, True, me - 1).start()

        @pl.when(me < PARTS - 1)
        def _():
            face_copy(step, False, me + 1).start()

        for h in range(2):
            collect(h, out1, in1, s1, r1)
            high, low = split(mm(member[...], xh[...]) + mm(member[...], xl[...]))
            applied = mm(cbh[...], high) + (mm(cbh[...], low) + mm(cbl[...], high))
            high, low = split(applied)

            @pl.when(step > 0)
            def _():
                sent(h, out2, in2, s2, r2)

            exchange(h, lambda at: mm(memt[at, :], high) + mm(memt[at, :], low), out2, in2, s2, r2)

        @pl.when(me > 0)
        def _():
            face_wait(step, True, me - 1).wait()

        @pl.when(me < PARTS - 1)
        def _():
            face_wait(step, False, me + 1).wait()

        high, low = split(face_in[step])
        gh[0 : 2 * FACE, :] = high
        gl[0 : 2 * FACE, :] = low

        def assemble(i):
            at = rows_at(i, 512)
            summed = cells[at, :] + mm(fsca[at, :], gh[0:256, :]) + mm(fsca[at, :], gl[0:256, :])
            field = filtered[at, :]
            cells[at, :] = (summed - centre * field) * gain - keep * previous[at, :]
            previous[at, :] = field

        loop(NODES // 512, assemble)
        for h in range(2):
            columns = sides(h)
            collect(h, out2, in2, s2, r2)
            bh, bl = split(mm(placet[...], xh[...]) + mm(placet[...], xl[...]))

            def finish(i):
                at = rows_at(i, 512)
                back = mm(b24th[at, :], bh) + (mm(b24th[at, :], bl) + mm(b24tl[at, :], bh))
                field = cells[at, columns] + gain * back
                filtered[at, columns] = field
                high, low = split(field)
                vh[at, columns] = high
                vl[at, columns] = low

            loop(NODES // 512, finish)
            sent(h, out1, in1, s1, r1)

            @pl.when(step < 2)
            def _():
                send_coefficients(h)

            @pl.when(step == 2)
            def _():
                def begin(t):
                    i = lax.rem(t + me // 2, GROUPS)

                    @pl.when(i > 0)
                    def _():
                        half_of(i, h, me, band, filtered, halves, sh, rh).start()

                loop(GROUPS, begin)
                for i in range(NODES // BLOCK):
                    at = slice(i * BLOCK, (i + 1) * BLOCK)
                    high, low = split(filtered[at, columns].T * node_weight[:, at])
                    wth[columns, at] = high
                    wtl[columns, at] = low

    loop(3, degree)
    for h in range(2):
        sent(h, out2, in2, s2, r2)
    margin_of(
        me, band, other, quarter, node_weight, filtered, margin, vh, vl, wth, wtl, product, halves, kept, given, core_in, strips,
        turned, swapped, sh, rh, sc, rc, ss, rs, sw, rw,
    )


def choose(i, values):
    result = values[0]
    for k in range(1, GROUPS):
        result = jnp.where(i == k, values[k], result)
    return result


def apart(i):
    return choose(i, (0, 0, 1, 3, 1, 3, 2, 2)), choose(i, (0, 1, 0, 0, 1, 1, 0, 1))


def group_at(band, dy, dx):
    return lax.rem(band // 2 + dy, 4) * 2 + lax.rem(band + dx, 2)


def half_of(i, h, me, band, filtered, halves, sh, rh):
    x, far = lax.rem(band, 2), band // 4
    mine = choose(i, (0, x, 0, 1, 0, 1, far, far))
    columns = pl.ds(h * 128, 128)
    return pltpu.make_async_remote_copy(
        filtered.at[rows_at(mine, NODES // 2), columns],
        halves.at[i - 1, :, columns],
        sh.at[i - 1, h],
        rh.at[i - 1, h],
        device_id=(group_at(band, *apart(i)), me),
        device_id_type=MESH,
    )


def margin_of(
    me, band, other, quarter, node_weight, filtered, margin, vh, vl, wth, wtl, product, halves, kept, given, core_in, strips,
    turned, swapped, sh, rh, sc, rc, ss, rs, sw, rw,
):
    x, far = lax.rem(band, 2), band // 4
    core, chip = lax.rem(me, 2), me // 2
    sibling = me + 1 - 2 * core

    def block_at(t):
        return lax.rem(t + chip, GROUPS)

    def owner(i):
        dy, dx = apart(i)
        return group_at(band, 4 - dy, dx)

    def half_copy(i, h):
        return half_of(i, h, me, band, filtered, halves, sh, rh)

    def core_copy(i, j):
        return pltpu.make_async_remote_copy(
            given.at[i, j], core_in.at[i, j], sc.at[i, j], rc.at[i, j], device_id=(band, sibling), device_id_type=MESH
        )

    def strip_copy(i, j, target):
        return pltpu.make_async_remote_copy(
            kept.at[i, j], strips.at[chip], ss.at[i, j], rs.at[chip], device_id=(band, target), device_id_type=MESH
        )

    lower = iota((128, 128), 1) < 64

    def send_strips(i, j):
        core_copy(i, j).wait_recv()
        kept[i, j] = kept[i, j] + core_in[i, j]
        target = owner(i) * 4 + 2 * j + core

        @pl.when(target == me)
        def _():
            strips[chip] = kept[i, j]

        @pl.when(target != me)
        def _():
            strip_copy(i, j, target).start()

    def multiply(t, j):
        i = block_at(t)
        columns = slice(j * 128, (j + 1) * 128)

        @pl.when(i == 0)
        def _():
            high, low = vh[:, columns], vl[:, columns]
            product[...] = mm(wth[...], high) + (mm(wth[...], low) + mm(wtl[...], high))

        @pl.when(i > 0)
        def _():
            half_copy(i, j).wait_recv()
            at = rows_at(choose(i, (0, 1 - x, 0, 1, 0, 1, 1 - far, 1 - far)), NODES // 2)
            high, low = split(halves[i - 1, :, columns])
            product[...] = mm(wth[:, at], high) + (mm(wth[:, at], low) + mm(wtl[:, at], high))

        top, bottom = product[:128, :], product[128:, :]
        even = jnp.where(lower, top, pltpu.roll(bottom, 64, 1))
        odd = jnp.where(lower, pltpu.roll(top, 64, 1), bottom)
        kept[i, j] = jnp.where(core == 0, even, odd)
        given[i, j] = jnp.where(core == 0, odd, even)
        core_copy(i, j).start()

        @pl.when(t > 0)
        def _():
            send_strips(block_at(t + GROUPS - 1), j)

    for j in range(2):
        loop(GROUPS, lambda t: multiply(t, j))
        send_strips(block_at(GROUPS - 1), j)

    def arrived(k):
        source = lax.rem(chip + k + 1, PARTS // 2)
        pltpu.make_async_remote_copy(
            kept.at[0, 0], strips.at[source], ss.at[0, 0], rs.at[source], device_id=(band, source * 2 + core), device_id_type=MESH
        ).wait_recv()

    loop(PARTS // 2 - 1, arrived)
    total = jnp.sum(strips[...], axis=0)
    flipped = total.T
    margin[:, :128] = flipped[:64]
    margin[:, 128:] = flipped[64:]

    def swap_copy(j):
        return pltpu.make_async_remote_copy(
            turned.at[pl.ds(64 * (j % 2), 64)],
            swapped.at[quarter],
            sw.at[j],
            rw.at[quarter],
            device_id=(other, band * 4 + j),
            device_id_type=MESH,
        )

    @pl.when(other != band)
    def _():
        turned[...] = total
        for j in range(4):
            swap_copy(j).start()
        for j in range(4):
            pltpu.make_async_remote_copy(
                turned.at[pl.ds(0, 64)], swapped.at[j], sw.at[j], rw.at[j], device_id=(other, band * 4 + j), device_id_type=MESH
            ).wait_recv()
        lowest = iota((64, 128), 1) < 64
        for j in range(2):
            even, odd = swapped[2 * j], swapped[2 * j + 1]
            left = jnp.where(lowest, even, pltpu.roll(odd, 64, 1))
            right = jnp.where(lowest, pltpu.roll(even, 64, 1), odd)
            margin[:, j * 128 : (j + 1) * 128] += jnp.where(quarter < 2, left, right)
        for j in range(4):
            swap_copy(j).wait_send()

    def finished(i):
        @pl.when(i > 0)
        def _():
            for h in range(2):
                half_copy(i, h).wait_send()

        for j in range(2):
            core_copy(i, j).wait_send()
            target = owner(i) * 4 + 2 * j + core

            @pl.when(target != me)
            def _():
                strip_copy(i, j, target).wait_send()

    loop(GROUPS, finished)


def run_filter(
    bands_in, cell_ham, cell_nodes, left_face, right_face, proj_values, proj_nodes, slot_owner, slot_atom, coupling, node_weight,
    filter_center, filter_half,
):
    vmem = pl.BlockSpec(memory_space=pltpu.VMEM)
    smem = pl.BlockSpec(memory_space=pltpu.SMEM)
    D = pltpu.SemaphoreType.DMA
    V = pltpu.VMEM
    slot_rows = SLOTS * PADDED
    pairs = D((2, PARTS))
    filtered, margin = pl.pallas_call(
        filter_kernel,
        out_shape=(jax.ShapeDtypeStruct((NODES, COLS), f32), jax.ShapeDtypeStruct((64, COLS), f32)),
        in_specs=[smem] * 2 + [vmem] * 11,
        out_specs=(vmem, vmem),
        scratch_shapes=[
            V((slot_rows, 128), f32),
            V((TERMS, 128), f32),
            V((slot_rows, NODES), f32),
            V((slot_rows, NODES), bf16),
            V((slot_rows, NODES), bf16),
            V((NODES, slot_rows), bf16),
            V((NODES, slot_rows), bf16),
            V((ROWS, slot_rows), bf16),
            V((slot_rows, ROWS), bf16),
            V((CELLS * CELL, NODES), bf16),
            V((NODES, CELLS * CELL), bf16),
            V((2 * FACE, NODES), bf16),
            V((NODES, 2 * FACE), bf16),
            V((TERMS, ROWS), bf16),
            V((ROWS, TERMS), bf16),
            V((TERMS, TERMS), bf16),
            V((TERMS, TERMS), bf16),
            V((NODES, COLS), bf16),
            V((NODES, COLS), bf16),
            V((ROWS, 128), bf16),
            V((ROWS, 128), bf16),
            V((CELLS * CELL, COLS), bf16),
            V((CELLS * CELL, COLS), bf16),
            V((CELLS * CELL, COLS), bf16),
            V((CELLS * CELL, COLS), bf16),
            V((NODES, COLS), f32),
            V((NODES, COLS), f32),
            V((2, PARTS, WIDE, 128), f32),
            V((2, PARTS, WIDE, 128), f32),
            V((2, PARTS, WIDE, 128), f32),
            V((2, PARTS, WIDE, 128), f32),
            V((PARTS, 8, 128), f32),
            V((PARTS, 8, 128), f32),
            V((2 * FACE, COLS), f32),
            V((3, 2 * FACE, COLS), f32),
            pairs,
            pairs,
            pairs,
            pairs,
            D((PARTS,)),
            D((PARTS,)),
            D((2,)),
            D((3, 2)),
            V((COLS, NODES), bf16),
            V((COLS, NODES), bf16),
            V((COLS, 128), f32),
            V((7, NODES // 2, COLS), f32),
            V((GROUPS, 2, 128, 128), f32),
            V((GROUPS, 2, 128, 128), f32),
            V((GROUPS, 2, 128, 128), f32),
            V((PARTS // 2, 128, 128), f32),
            V((128, 128), f32),
            V((4, 64, 128), f32),
            D((7, 2)),
            D((7, 2)),
            D((GROUPS, 2)),
            D((GROUPS, 2)),
            D((GROUPS, 2)),
            D((PARTS // 2,)),
            D((4,)),
            D((4,)),
        ],
        compiler_params=pltpu.CompilerParams(
            collective_id=0, has_side_effects=True, vmem_limit_bytes=58 * 2**20
        ),
        name="filter_bands",
    )(
        filter_center,
        filter_half,
        bands_in,
        cell_ham,
        cell_nodes,
        left_face,
        right_face,
        jnp.transpose(proj_values, (1, 0, 2)),
        proj_nodes,
        slot_owner.reshape(1, SLOTS),
        slot_atom.reshape(1, SLOTS),
        jnp.transpose(coupling, (1, 0, 2)),
        node_weight.reshape(1, NODES),
    )
    return filtered, margin.T


def per_device(
    bands_in,
    cell_ham,
    cell_nodes,
    left_face,
    right_face,
    proj_values,
    proj_nodes,
    slot_owner,
    slot_atom,
    coupling,
    node_weight,
    filter_center,
    filter_half,
):
    return run_filter(
        bands_in, cell_ham, cell_nodes, left_face, right_face, proj_values, proj_nodes, slot_owner, slot_atom, coupling,
        node_weight, filter_center, filter_half,
    )


def solution(mesh):
    placed = (
        P("mesh", "band"),
        P("mesh", None, None),
        P("mesh", None),
        P("mesh", None),
        P("mesh", None),
        P("mesh", None, None),
        P("mesh", None),
        P("mesh", None),
        P("mesh"),
        P("mesh", None, None),
        P("mesh"),
        P(),
        P(),
    )
    return jax.shard_map(
        per_device,
        mesh=mesh,
        in_specs=placed,
        out_specs=(P("mesh", "band"), P("band", "mesh")),
        check_vma=False,
    )
```
